32 devices in a mesh: dp: 8 (over z, x), zero: 4 (over y, core).
Axes of the slice: x: 2, y: 2, z: 4, core: 2. Of those that a mesh axis runs over, the one named last changes fastest.
Arguments:
- grad_parts: bfloat16 [8, 3, 704, 1024], P('dp', None, 'zero'), may hold values from -1.5 to 1.5
- momentum: float32 [3, 704, 1024], P(None, 'zero')
- owner_table: int32 [3], replicated, may hold values from 0 to 3, as said below
Outputs:
- new_momentum: float32 [3, 704, 1024], P(None, 'zero')
- update: bfloat16 [3, 704, 1024], P(None, 'zero')
- owner_copy: bfloat16 [4, 704, 1024], P('zero')
The draws below stay inside these ranges and needn't reach their ends.
Inputs may be any that keep to these rules, and one draw needn't show every extreme that they name: `owner_table`: the 3 entries are distinct; the first and the last device along zero always own a matrix.
All inputs are finite; a program needn't handle non-finite values.
Results may differ from the reference program's by a relative error of at most 0.0062.
Values may be sent and summed in bfloat16 or wider, within the bound.
A program may use at most 64 MiB of HBM per device.

```python
import math
import jax
import jax.numpy as jnp
from jax import lax

D = 1024
HID = 704
MATS = 3
ITERS = 2
N_DP = 8
N_ZERO = 4


def draw_momentum(key, part):
    key_base, key_row, key_col = jax.random.split(key, 3)
    place = jnp.arange(HID, dtype=jnp.float32) / max(HID - 1, 1)
    trend = jnp.exp(math.log(3.0) * place)
    row_scale = jnp.exp(jax.random.uniform(key_row, (HID,), minval=0.0, maxval=math.log(10.0)))
    col_scale = jnp.exp(jax.random.uniform(key_col, (D,), minval=0.0, maxval=math.log(10.0)))
    base = jax.random.normal(key_base, (MATS, HID, D))
    factor = 0.05
    scaled = base * (trend * row_scale)[None, :, None] * col_scale[None, None, :] * factor
    return scaled.astype(jnp.float32)


def distinct_order(key, count):
    scores = jax.random.randint(key, (count,), 0, 1048576, dtype=jnp.int32) * count + jnp.arange(count, dtype=jnp.int32)
    return jnp.argsort(scores, stable=True).astype(jnp.int32)


def draw_owner_table(key, part):
    key_middle = jax.random.fold_in(key, 7101)
    key_order = jax.random.fold_in(key, 7202)
    middle = distinct_order(key_middle, N_ZERO - 2) + 1
    ends = jnp.array([0, N_ZERO - 1], dtype=jnp.int32)
    owners = jnp.concatenate([ends, middle.astype(jnp.int32)])[:MATS]
    order = distinct_order(key_order, MATS)
    return owners[order].astype(jnp.int32)


def levels(stream_key, extent, shards, low, largest):
    loudness = 1.0
    for position, parts in shards:
        draws = jax.random.uniform(jax.random.fold_in(jax.random.fold_in(stream_key, 6), position), (parts,), jnp.float32, low / len(shards), largest / len(shards))
        loudness = loudness * jnp.repeat(jnp.exp(draws), extent[position] // parts).reshape((-1,) + (1,) * (len(extent) - 1 - position))
    return loudness


def normal_values(own_key, shape, scale, reach, cuts=(), held_as=jnp.bfloat16):
    drawn = scale * jax.random.normal(own_key, shape, jnp.float32)
    if cuts:
        drawn = drawn * levels(own_key, shape, cuts, -0.22, 0.18)
    return jnp.clip(drawn, -reach, reach).astype(held_as)


def setup_inputs(seed: int = 0) -> dict:
    key_list = jax.random.split(jax.random.key(seed), 4)
    grad_parts = normal_values(key_list[0], (N_DP, MATS, HID, D), 0.1, 1.5, ((0, 8), (2, 4)))
    momentum = draw_momentum(jax.random.fold_in(key_list[3], 71), 0)
    owner_table = draw_owner_table(jax.random.fold_in(key_list[3], 71), 0)
    return {"grad_parts": grad_parts, "momentum": momentum, "owner_table": owner_table}


COEF_A = 3.4445
COEF_B = -4.775
COEF_C = 2.0315
MOMENTUM_DECAY = 0.95
NORM_EPSILON = 1e-07

def orthogonalize(matrix):
    current = matrix
    iterate = matrix.astype(jnp.float32)
    for step in range(ITERS):
        gram_matrix = jnp.dot(current, current.T, preferred_element_type=jnp.float32).astype(jnp.bfloat16)
        squared = jnp.dot(gram_matrix, gram_matrix, preferred_element_type=jnp.float32)
        poly_term = (COEF_B * gram_matrix.astype(jnp.float32) + COEF_C * squared).astype(jnp.bfloat16)
        iterate = COEF_A * current.astype(jnp.float32) + jnp.dot(poly_term, current, preferred_element_type=jnp.float32)
        if step + 1 < ITERS:
            current = iterate.astype(jnp.bfloat16)
    return (0.2 * math.sqrt(D) * iterate).astype(jnp.bfloat16)

def add_replica(running, replica):
    return (running + replica.astype(jnp.float32), None)

def reference(grad_parts, momentum, owner_table):
    summed, _ = lax.scan(add_replica, jnp.zeros(grad_parts.shape[1:], jnp.float32), grad_parts)
    new_momentum = MOMENTUM_DECAY * momentum + summed
    norms = jnp.sqrt(lax.optimization_barrier(jnp.sum(new_momentum * new_momentum, axis=(1, 2))))
    start_rows = (new_momentum / (norms[:, None, None] + NORM_EPSILON)).astype(jnp.bfloat16)
    update = lax.map(orthogonalize, start_rows)
    onehot = (owner_table[None, :] == jnp.arange(N_ZERO, dtype=jnp.int32)[:, None]).astype(jnp.float32)
    owner_copy = jnp.einsum('oj,jrd->ord', onehot, update.astype(jnp.float32)).astype(jnp.bfloat16)
    return (new_momentum, update, owner_copy)
```

```python
import math

import jax
import jax.numpy as jnp
from jax import lax
from jax.experimental import pallas as pl
from jax.experimental.pallas import tpu as pltpu
from jax.sharding import PartitionSpec as P

ITERS = 2
COEF_A = 3.4445
COEF_B = -4.775
COEF_C = 2.0315
MOMENTUM_DECAY = 0.95
NORM_EPSILON = 1e-07
MESH = pl.DeviceIdType.MESH
LANES = 128


def orthogonalize(matrix):
    current = matrix
    iterate = matrix.astype(jnp.float32)
    for step in range(ITERS):
        gram_matrix = jnp.dot(current, current.T, preferred_element_type=jnp.float32).astype(
            jnp.bfloat16
        )
        squared = jnp.dot(gram_matrix, gram_matrix, preferred_element_type=jnp.float32)
        poly_term = (COEF_B * gram_matrix.astype(jnp.float32) + COEF_C * squared).astype(
            jnp.bfloat16
        )
        iterate = COEF_A * current.astype(jnp.float32) + jnp.dot(
            poly_term, current, preferred_element_type=jnp.float32
        )
        if step + 1 < ITERS:
            current = iterate.astype(jnp.bfloat16)
    return (0.2 * math.sqrt(matrix.shape[1]) * iterate).astype(jnp.bfloat16)


def general_step(grad_parts, momentum, owner_table):
    my_index = lax.axis_index("zero")
    local_part = grad_parts[0].astype(jnp.float32)
    summed = lax.psum(local_part, "dp")
    new_momentum = MOMENTUM_DECAY * momentum + summed
    partial_value = jnp.sum(new_momentum * new_momentum, axis=(1, 2))
    squares = lax.psum(partial_value, "zero")
    inverse = 1.0 / (jnp.sqrt(squares) + NORM_EPSILON)
    start_rows = (new_momentum * inverse[:, None, None]).astype(jnp.bfloat16)
    mine_mask = (owner_table == my_index).astype(jnp.bfloat16)
    gathered = lax.all_gather(start_rows, "zero", axis=1, tiled=True)
    full_matrix = jnp.einsum(
        "j,jrd->rd", mine_mask, gathered, preferred_element_type=jnp.float32
    ).astype(jnp.bfloat16)
    result = orthogonalize(full_matrix)
    contrib = mine_mask.astype(jnp.float32)[:, None, None] * result.astype(jnp.float32)[None]
    update_rows = lax.psum_scatter(
        contrib.astype(jnp.bfloat16), "zero", scatter_dimension=1, tiled=True
    )
    return (new_momentum, update_rows, result[None])


def column_tiles(width, step=256):
    return [(at, min(step, width - at)) for at in range(0, width, step)]


def make_kernel(n_dp, n_zero, mats, rows, dim):
    hid = rows * n_zero
    n_line = n_dp // 2
    width = dim // n_dp
    out_scale = 0.2 * math.sqrt(dim)

    def kernel(
        grad, momentum, nm_out, up_out,
        x, parts, mom, gram, poly, scale,
        rs_s, rs_r, s1_s, s1_r, s2_s, s2_r, s3_s, s3_r, s4_s, s4_r, local,
    ):
        d = lax.axis_index("dp")
        o = lax.axis_index("zero")
        zi, xi, yi, ci = d // 2, d % 2, o // 2, o % 2
        x_peer = zi * 2 + 1 - xi
        y_peer = (1 - yi) * 2 + ci
        c_peer = yi * 2 + 1 - ci

        def row(s):
            return pl.ds(pl.multiple_of(s * rows, 16), rows)

        def col(k):
            return pl.ds(pl.multiple_of(k * width, LANES), width)

        def chunk(j, s, k):
            return x.at[j, row(s), col(k)]

        def line(r):
            return (zi + n_line - r) % n_line

        def remote(src, dst, send, recv, to):
            return pltpu.make_async_remote_copy(
                src_ref=src, dst_ref=dst, send_sem=send, recv_sem=recv,
                device_id=to, device_id_type=MESH,
            )

        def rs(j, r):
            p = (d + r) % n_dp
            return remote(grad.at[0, j, :, col(p)], parts.at[j, r], rs_s.at[j, r], rs_r.at[j, r], (p, o))

        def s1(j, r):
            c = chunk(j, o, d)
            return remote(c, c, s1_s.at[j, r], s1_r.at[j, r], (((zi + r) % n_line) * 2 + xi, o))

        def s1_in(j, r):
            c = chunk(j, o, line(r) * 2 + xi)
            return remote(c, c, s1_s.at[j, r], s1_r.at[j, r], (((zi + r) % n_line) * 2 + xi, o))

        def s2(j, r):
            c = chunk(j, o, line(r) * 2 + xi)
            return remote(c, c, s2_s.at[j, r], s2_r.at[j, r], (x_peer, o))

        def s2_in(j, r):
            c = chunk(j, o, line(r) * 2 + 1 - xi)
            return remote(c, c, s2_s.at[j, r], s2_r.at[j, r], (x_peer, o))

        def s3(j, r, h, s=None):
            k = line(r) * 2 + (xi if h == 0 else 1 - xi)
            c = chunk(j, o if s is None else s, k)
            return remote(c, c, s3_s.at[j, r, h], s3_r.at[j, r, h], (d, y_peer))

        def s3_in(j, r, h):
            return s3(j, r, h, y_peer)

        def s4(j, h, s=None):
            if s is None:
                s = o if h == 0 else y_peer
            c = x.at[j, row(s), :]
            return remote(c, c, s4_s.at[j, h], s4_r.at[j, h], (d, c_peer))

        def s4_in(j, h):
            return s4(j, h, c_peer if h == 0 else (1 - yi) * 2 + 1 - ci)

        def own_part(j):
            return pltpu.make_async_copy(grad.at[0, j, :, col(d)], parts.at[j, 0], local.at[j])

        def own_momentum():
            return pltpu.make_async_copy(momentum.at[:, :, col(d)], mom, local.at[mats])

        def nm_copy(j):
            return pltpu.make_async_copy(x.at[j, row(o), :], nm_out.at[j], local.at[mats + 1 + j])

        def up_copy(j):
            return pltpu.make_async_copy(x.at[j], up_out.at[j], local.at[2 * mats + 1 + j])

        peers = [((d + r) % n_dp, o) for r in range(1, n_dp)] + [(d, y_peer), (d, c_peer)]
        barrier = pltpu.get_barrier_semaphore()
        own_momentum().start()
        for j in range(mats):
            own_part(j).start()
        for to in peers:
            pl.semaphore_signal(barrier, inc=1, device_id=to, device_id_type=MESH)
        pl.semaphore_wait(barrier, len(peers))
        for j in range(mats):
            for r in range(1, n_dp):
                rs(j, r).start()

        def phase_a(j):
            if j == 0:
                own_momentum().wait()
            own_part(j).wait()
            for r in range(1, n_dp):
                rs(j, r).wait_recv()
            total = parts[j, 0].astype(jnp.float32)
            for r in range(1, n_dp):
                total = total + parts[j, r].astype(jnp.float32)
            x[j, row(o), col(d)] = (MOMENTUM_DECAY * mom[j] + total).astype(jnp.bfloat16)
            s3(j, 0, 0).start()
            s2(j, 0).start()
            for r in range(1, n_line):
                s1(j, r).start()

        def phase_b(j):
            for r in range(1, n_line):
                s1_in(j, r).wait_recv()
                s2(j, r).start()
                s3(j, r, 0).start()

        def phase_c(j):
            for r in range(n_line):
                s2_in(j, r).wait_recv()
                s3(j, r, 1).start()
            s4(j, 0).start()
            nm_copy(j).start()

        def phase_d(j):
            for r in range(n_line):
                for h in range(2):
                    s3_in(j, r, h).wait_recv()
            s4(j, 1).start()

        def phase_e(j):
            for h in range(2):
                s4_in(j, h).wait_recv()
            for r in range(1, n_dp):
                rs(j, r).wait_send()
            for r in range(1, n_line):
                s1(j, r).wait_send()
            for r in range(n_line):
                s2(j, r).wait_send()
                for h in range(2):
                    s3(j, r, h).wait_send()
            for h in range(2):
                s4(j, h).wait_send()
            nm_copy(j).wait()

        def ns_step(t):
            j, it = t // ITERS, t % ITERS

            @pl.when(it == 0)
            def _():
                def add(i, acc):
                    v = x[j, pl.ds(pl.multiple_of(i * 16, 16), 16), :].astype(jnp.float32)
                    return acc + v * v

                acc = lax.fori_loop(0, hid // 16, add, jnp.zeros((16, dim), jnp.float32))
                total = jnp.sum(jnp.sum(acc, axis=0, keepdims=True), axis=1, keepdims=True)
                scale[...] = jnp.broadcast_to(1.0 / (jnp.sqrt(total) + NORM_EPSILON), scale.shape)

            @pl.when(it != 0)
            def _():
                scale[...] = jnp.ones(scale.shape, jnp.float32)

            s = scale[0:1, 0:1]
            for at, size in column_tiles(hid):
                g = lax.dot_general(
                    x[j], x[j, at : at + size, :], (((1,), (1,)), ((), ())),
                    preferred_element_type=jnp.float32,
                )
                gram[:, at : at + size] = (g * s * s).astype(jnp.bfloat16)
            for at, size in column_tiles(hid):
                block = gram[:, at : at + size]
                q = jnp.dot(gram[...], block, preferred_element_type=jnp.float32)
                poly[:, at : at + size] = (COEF_B * block.astype(jnp.float32) + COEF_C * q).astype(
                    jnp.bfloat16
                )
            last = (it == ITERS - 1).astype(jnp.float32)
            post = s * (1.0 + last * (out_scale - 1.0))

            def apply(i, carry):
                cols = pl.ds(pl.multiple_of(i * 256, 256), 256)
                block = x[j, :, cols]
                y = COEF_A * block.astype(jnp.float32) + jnp.dot(
                    poly[...], block, preferred_element_type=jnp.float32
                )
                x[j, :, cols] = (y * post).astype(jnp.bfloat16)
                return carry

            lax.fori_loop(0, dim // 256, apply, 0)

        phase_a(0)
        phase_b(0)
        phase_c(0)
        phase_a(1)
        phase_d(0)
        phase_b(1)
        phase_c(1)
        phase_e(0)

        def step(t, carry):
            ns_step(t)

            @pl.when(t == 0)
            def _():
                phase_a(2)
                phase_b(2)

            @pl.when(t == 1)
            def _():
                up_copy(0).start()
                phase_c(2)
                phase_d(1)
                phase_e(1)

            @pl.when(t == 2)
            def _():
                phase_d(2)

            @pl.when(t == 3)
            def _():
                up_copy(1).start()
                phase_e(2)

            return carry

        lax.fori_loop(0, mats * ITERS, step, 0)
        up_copy(2).start()
        for j in range(mats):
            up_copy(j).wait()

    dma = pltpu.SemaphoreType.DMA
    flops = mats * ITERS * 2 * hid * hid * (2 * dim + hid)
    return pl.pallas_call(
        kernel,
        out_shape=(
            jax.ShapeDtypeStruct((mats, rows, dim), jnp.bfloat16),
            jax.ShapeDtypeStruct((mats, hid, dim), jnp.bfloat16),
        ),
        in_specs=[pl.BlockSpec(memory_space=pl.ANY)] * 2,
        out_specs=(pl.BlockSpec(memory_space=pl.ANY),) * 2,
        scratch_shapes=[
            pltpu.VMEM((mats, hid, dim), jnp.bfloat16),
            pltpu.VMEM((mats, n_dp, rows, width), jnp.bfloat16),
            pltpu.VMEM((mats, rows, width), jnp.float32),
            pltpu.VMEM((hid, hid), jnp.bfloat16),
            pltpu.VMEM((hid, hid), jnp.bfloat16),
            pltpu.VMEM((8, LANES), jnp.float32),
            dma((mats, n_dp)), dma((mats, n_dp)),
            dma((mats, n_line)), dma((mats, n_line)),
            dma((mats, n_line)), dma((mats, n_line)),
            dma((mats, n_line, 2)), dma((mats, n_line, 2)),
            dma((mats, 2)), dma((mats, 2)),
            dma((3 * mats + 1,)),
        ],
        cost_estimate=pl.CostEstimate(flops=flops, bytes_accessed=16 * mats * rows * dim, transcendentals=0),
        compiler_params=pltpu.CompilerParams(
            collective_id=0, has_side_effects=True, vmem_limit_bytes=40 * 1024 * 1024
        ),
    )


def solution(mesh):
    n_dp, n_zero = mesh.shape["dp"], mesh.shape["zero"]

    def kernel_step(grad_parts, momentum, owner_table):
        _, mats, rows, dim = grad_parts.shape
        me = lax.axis_index("zero")
        nm, update = make_kernel(n_dp, n_zero, mats, rows, dim)(grad_parts, momentum)
        mine = owner_table == me
        which = jnp.argmax(mine)
        copy = lax.dynamic_index_in_dim(update, which, 0, keepdims=True)
        copy = jnp.where(jnp.any(mine), copy, jnp.zeros_like(copy))
        update_rows = lax.dynamic_slice_in_dim(update, me * rows, rows, axis=1)
        return nm.astype(jnp.float32), update_rows, copy

    def on_device(grad_parts, momentum, owner_table):
        _, mats, rows, dim = grad_parts.shape
        fits = (
            mats == 3
            and n_zero == 4
            and n_dp % 2 == 0
            and n_dp >= 4
            and dim % (LANES * n_dp) == 0
            and dim % 256 == 0
            and rows % 16 == 0
        )
        body = kernel_step if fits else general_step
        return body(grad_parts, momentum, owner_table)

    placed = (P("dp", None, "zero", None), P(None, "zero", None), P())
    return jax.shard_map(
        on_device,
        mesh=mesh,
        in_specs=placed,
        out_specs=(P(None, "zero", None), P(None, "zero", None), P("zero", None, None)),
        check_vma=False,
    )
```

```python
import math

import jax
import jax.numpy as jnp
from jax import lax
from jax.experimental import pallas as pl
from jax.experimental.pallas import tpu as pltpu
from jax.sharding import PartitionSpec as P

ITERS = 2
COEF_A = 3.4445
COEF_B = -4.775
COEF_C = 2.0315
MOMENTUM_DECAY = 0.95
NORM_EPSILON = 1e-07
MESH = pl.DeviceIdType.MESH
LANES = 128


def orthogonalize(matrix):
    current = matrix
    iterate = matrix.astype(jnp.float32)
    for step in range(ITERS):
        gram_matrix = jnp.dot(current, current.T, preferred_element_type=jnp.float32).astype(
            jnp.bfloat16
        )
        squared = jnp.dot(gram_matrix, gram_matrix, preferred_element_type=jnp.float32)
        poly_term = (COEF_B * gram_matrix.astype(jnp.float32) + COEF_C * squared).astype(
            jnp.bfloat16
        )
        iterate = COEF_A * current.astype(jnp.float32) + jnp.dot(
            poly_term, current, preferred_element_type=jnp.float32
        )
        if step + 1 < ITERS:
            current = iterate.astype(jnp.bfloat16)
    return (0.2 * math.sqrt(matrix.shape[1]) * iterate).astype(jnp.bfloat16)


def general_step(grad_parts, momentum, owner_table):
    my_index = lax.axis_index("zero")
    local_part = grad_parts[0].astype(jnp.float32)
    summed = lax.psum(local_part, "dp")
    new_momentum = MOMENTUM_DECAY * momentum + summed
    partial_value = jnp.sum(new_momentum * new_momentum, axis=(1, 2))
    squares = lax.psum(partial_value, "zero")
    inverse = 1.0 / (jnp.sqrt(squares) + NORM_EPSILON)
    start_rows = (new_momentum * inverse[:, None, None]).astype(jnp.bfloat16)
    mine_mask = (owner_table == my_index).astype(jnp.bfloat16)
    gathered = lax.all_gather(start_rows, "zero", axis=1, tiled=True)
    full_matrix = jnp.einsum(
        "j,jrd->rd", mine_mask, gathered, preferred_element_type=jnp.float32
    ).astype(jnp.bfloat16)
    result = orthogonalize(full_matrix)
    contrib = mine_mask.astype(jnp.float32)[:, None, None] * result.astype(jnp.float32)[None]
    update_rows = lax.psum_scatter(
        contrib.astype(jnp.bfloat16), "zero", scatter_dimension=1, tiled=True
    )
    return (new_momentum, update_rows, result[None])


def column_tiles(width, step=256):
    return [(at, min(step, width - at)) for at in range(0, width, step)]


def make_kernel(n_dp, n_zero, mats, rows, dim):
    hid = rows * n_zero
    half = hid // 2
    n_line = n_dp // 2
    width = dim // n_dp
    out_scale = 0.2 * math.sqrt(dim)

    def kernel(
        grad, momentum, nm_out, up_out,
        x, later, gram, parts, mom, poly, scale,
        rs_s, rs_r, s1_s, s1_r, s2_s, s2_r, s3_s, s3_r, s4_s, s4_r, gx_s, gx_r, xx_s, xx_r, local,
    ):
        d = lax.axis_index("dp")
        o = lax.axis_index("zero")
        zi, xi, yi, ci = d // 2, d % 2, o // 2, o % 2
        x_peer = zi * 2 + 1 - xi
        y_peer = (1 - yi) * 2 + ci
        c_peer = yi * 2 + 1 - ci

        def row(s):
            return pl.ds(pl.multiple_of(s * rows, 16), rows)

        def col(k):
            return pl.ds(pl.multiple_of(k * width, LANES), width)

        def chunk(j, s, k):
            return x.at[j, row(s), col(k)]

        def line(r):
            return (zi + n_line - r) % n_line

        def remote(src, dst, send, recv, to):
            return pltpu.make_async_remote_copy(
                src_ref=src, dst_ref=dst, send_sem=send, recv_sem=recv,
                device_id=to, device_id_type=MESH,
            )

        def rs(j, r):
            p = (d + r) % n_dp
            return remote(grad.at[0, j, :, col(p)], parts.at[j, r], rs_s.at[j, r], rs_r.at[j, r], (p, o))

        def s1(j, r):
            c = chunk(j, o, d)
            return remote(c, c, s1_s.at[j, r], s1_r.at[j, r], (((zi + r) % n_line) * 2 + xi, o))

        def s1_in(j, r):
            c = chunk(j, o, line(r) * 2 + xi)
            return remote(c, c, s1_s.at[j, r], s1_r.at[j, r], (((zi + r) % n_line) * 2 + xi, o))

        def s2(j, r):
            c = chunk(j, o, line(r) * 2 + xi)
            return remote(c, c, s2_s.at[j, r], s2_r.at[j, r], (x_peer, o))

        def s2_in(j, r):
            c = chunk(j, o, line(r) * 2 + 1 - xi)
            return remote(c, c, s2_s.at[j, r], s2_r.at[j, r], (x_peer, o))

        def s3(j, r, h, s=None):
            k = line(r) * 2 + (xi if h == 0 else 1 - xi)
            c = chunk(j, o if s is None else s, k)
            return remote(c, c, s3_s.at[j, r, h], s3_r.at[j, r, h], (d, y_peer))

        def s3_in(j, r, h):
            return s3(j, r, h, y_peer)

        def s4(j, h, s=None):
            if s is None:
                s = o if h == 0 else y_peer
            c = x.at[j, row(s), :]
            return remote(c, c, s4_s.at[j, h], s4_r.at[j, h], (d, c_peer))

        def s4_in(j, h):
            return s4(j, h, c_peer if h == 0 else (1 - yi) * 2 + 1 - ci)

        def own_part(j):
            return pltpu.make_async_copy(grad.at[0, j, :, col(d)], parts.at[j, 0], local.at[j])

        def own_momentum():
            return pltpu.make_async_copy(momentum.at[:, :, col(d)], mom, local.at[mats])

        def nm_copy(j):
            return pltpu.make_async_copy(x.at[j, row(o), :], nm_out.at[j], local.at[mats + 1 + j])

        def up_copy(j):
            return pltpu.make_async_copy(later.at[ITERS - 1, j], up_out.at[j], local.at[2 * mats + 1 + j])

        peers = [((d + r) % n_dp, o) for r in range(1, n_dp)] + [(d, y_peer), (d, c_peer)]
        barrier = pltpu.get_barrier_semaphore()
        own_momentum().start()
        for j in range(mats):
            own_part(j).start()
        for to in peers:
            pl.semaphore_signal(barrier, inc=1, device_id=to, device_id_type=MESH)
        pl.semaphore_wait(barrier, len(peers))
        for j in range(mats):
            for r in range(1, n_dp):
                rs(j, r).start()

        def phase_a(j):
            if j == 0:
                own_momentum().wait()
            own_part(j).wait()
            for r in range(1, n_dp):
                rs(j, r).wait_recv()
            total = parts[j, 0].astype(jnp.float32)
            for r in range(1, n_dp):
                total = total + parts[j, r].astype(jnp.float32)
            x[j, row(o), col(d)] = (MOMENTUM_DECAY * mom[j] + total).astype(jnp.bfloat16)
            s3(j, 0, 0).start()
            s2(j, 0).start()
            for r in range(1, n_line):
                s1(j, r).start()

        def phase_b(j):
            for r in range(1, n_line):
                s1_in(j, r).wait_recv()
                s2(j, r).start()
                s3(j, r, 0).start()

        def phase_c(j):
            for r in range(n_line):
                s2_in(j, r).wait_recv()
                s3(j, r, 1).start()
            s4(j, 0).start()
            nm_copy(j).start()

        def phase_d(j):
            for r in range(n_line):
                for h in range(2):
                    s3_in(j, r, h).wait_recv()
            s4(j, 1).start()

        def phase_e(j):
            for h in range(2):
                s4_in(j, h).wait_recv()

        def half_rows(c):
            return pl.ds(pl.multiple_of(c * half, 16), half)

        def gx(j, it, c=None):
            g = gram.at[j, it, half_rows(ci if c is None else c), :]
            return remote(g, g, gx_s.at[j, it], gx_r.at[j, it], (d, c_peer))

        def xx(j, it, c=None):
            v = later.at[it, j, half_rows(ci if c is None else c), :]
            return remote(v, v, xx_s.at[j, it], xx_r.at[j, it], (d, c_peer))

        mine = half_rows(ci)

        def source(j, it):
            return x.at[j] if it == 0 else later.at[it - 1, j]

        def gram_op(j, it):
            src = source(j, it)
            if it == 0:

                def add(i, acc):
                    v = src[pl.ds(pl.multiple_of(i * 16, 16), 16), :].astype(jnp.float32)
                    return acc + v * v

                acc = lax.fori_loop(0, hid // 16, add, jnp.zeros((16, dim), jnp.float32))
                total = jnp.sum(jnp.sum(acc, axis=0, keepdims=True), axis=1, keepdims=True)
                scale[j] = jnp.broadcast_to(1.0 / (jnp.sqrt(total) + NORM_EPSILON), scale.shape[1:])
            else:
                xx(j, it - 1, 1 - ci).wait_recv()
            for at, size in column_tiles(hid):
                g = lax.dot_general(
                    src[mine, :], src[at : at + size, :], (((1,), (1,)), ((), ())),
                    preferred_element_type=jnp.float32,
                )
                if it == 0:
                    s = scale[j, 0:1, 0:1]
                    g = g * s * s
                gram[j, it, mine, at : at + size] = g.astype(jnp.bfloat16)
            gx(j, it).start()

        def apply_op(j, it):
            src = source(j, it)
            gx(j, it, 1 - ci).wait_recv()
            for at, size in column_tiles(hid):
                q = jnp.dot(
                    gram[j, it, mine, :], gram[j, it, :, at : at + size],
                    preferred_element_type=jnp.float32,
                )
                block = gram[j, it, mine, at : at + size].astype(jnp.float32)
                poly[:, at : at + size] = (COEF_B * block + COEF_C * q).astype(jnp.bfloat16)

            def apply(i, carry):
                cols = pl.ds(pl.multiple_of(i * 256, 256), 256)
                y = COEF_A * src[mine, cols].astype(jnp.float32) + jnp.dot(
                    poly[...], src[:, cols], preferred_element_type=jnp.float32
                )
                if it == 0:
                    y = y * scale[j, 0:1, 0:1]
                if it == ITERS - 1:
                    y = y * out_scale
                later[it, j, mine, cols] = y.astype(jnp.bfloat16)
                return carry

            lax.fori_loop(0, dim // 256, apply, 0)
            xx(j, it).start()

        def finish(j):
            xx(j, ITERS - 1, 1 - ci).wait_recv()
            up_copy(j).start()

        phase_a(0)
        phase_b(0)
        phase_c(0)
        phase_a(1)
        phase_d(0)
        phase_b(1)
        phase_c(1)
        phase_e(0)
        gram_op(0, 0)
        phase_a(2)
        phase_b(2)
        apply_op(0, 0)
        gram_op(0, 1)
        phase_c(2)
        phase_d(1)
        phase_e(1)
        gram_op(1, 0)
        apply_op(0, 1)
        apply_op(1, 0)
        phase_d(2)
        phase_e(2)
        gram_op(2, 0)
        gram_op(1, 1)
        finish(0)
        apply_op(2, 0)
        apply_op(1, 1)
        gram_op(2, 1)
        finish(1)
        apply_op(2, 1)
        finish(2)

        for j in range(mats):
            for r in range(1, n_dp):
                rs(j, r).wait_send()
            for r in range(1, n_line):
                s1(j, r).wait_send()
            for r in range(n_line):
                s2(j, r).wait_send()
                for h in range(2):
                    s3(j, r, h).wait_send()
            for h in range(2):
                s4(j, h).wait_send()
            for it in range(ITERS):
                gx(j, it).wait_send()
                xx(j, it).wait_send()
            nm_copy(j).wait()
            up_copy(j).wait()

    dma = pltpu.SemaphoreType.DMA
    flops = mats * ITERS * hid * hid * (2 * dim + hid)
    return pl.pallas_call(
        kernel,
        out_shape=(
            jax.ShapeDtypeStruct((mats, rows, dim), jnp.bfloat16),
            jax.ShapeDtypeStruct((mats, hid, dim), jnp.bfloat16),
        ),
        in_specs=[pl.BlockSpec(memory_space=pl.ANY)] * 2,
        out_specs=(pl.BlockSpec(memory_space=pl.ANY),) * 2,
        scratch_shapes=[
            pltpu.VMEM((mats, hid, dim), jnp.bfloat16),
            pltpu.VMEM((ITERS, mats, hid, dim), jnp.bfloat16),
            pltpu.VMEM((mats, ITERS, hid, hid), jnp.bfloat16),
            pltpu.VMEM((mats, n_dp, rows, width), jnp.bfloat16),
            pltpu.VMEM((mats, rows, width), jnp.float32),
            pltpu.VMEM((half, hid), jnp.bfloat16),
            pltpu.VMEM((mats, 8, LANES), jnp.float32),
            dma((mats, n_dp)), dma((mats, n_dp)),
            dma((mats, n_line)), dma((mats, n_line)),
            dma((mats, n_line)), dma((mats, n_line)),
            dma((mats, n_line, 2)), dma((mats, n_line, 2)),
            dma((mats, 2)), dma((mats, 2)),
            dma((mats, ITERS)), dma((mats, ITERS)),
            dma((mats, ITERS)), dma((mats, ITERS)),
            dma((3 * mats + 1,)),
        ],
        cost_estimate=pl.CostEstimate(flops=flops, bytes_accessed=16 * mats * rows * dim, transcendentals=0),
        compiler_params=pltpu.CompilerParams(
            collective_id=0, has_side_effects=True, vmem_limit_bytes=58 * 1024 * 1024
        ),
    )


def make_finish(n_zero, mats, rows, dim):
    hid = rows * n_zero

    def kernel(table, nm, update, nm_out, up_out, own_out, nm_in, nm_wide, zeros, sems):
        me = lax.axis_index("zero")
        mine = update.at[:, pl.ds(pl.multiple_of(me * rows, 16), rows), :]
        nm_load = pltpu.make_async_copy(nm, nm_in, sems.at[2])
        nm_load.start()
        up_store = pltpu.make_async_copy(mine, up_out, sems.at[0])
        up_store.start()
        count = jnp.int32(0)
        for j in range(mats):
            owned = table[j] == me
            count = count + owned.astype(jnp.int32)

            @pl.when(owned)
            def _():
                pltpu.make_async_copy(update.at[j], own_out.at[0], sems.at[1]).start()

        @pl.when(count == 0)
        def _():
            zeros[...] = jnp.zeros(zeros.shape, zeros.dtype)
            pltpu.make_async_copy(zeros, own_out.at[0], sems.at[1]).start()

        nm_load.wait()
        for j in range(mats):
            nm_wide[j] = nm_in[j].astype(jnp.float32)
            pltpu.make_async_copy(nm_wide.at[j], nm_out.at[j], sems.at[3 + j]).start()
        up_store.wait()
        pltpu.make_async_copy(update.at[0], own_out.at[0], sems.at[1]).wait()
        for j in range(mats):
            pltpu.make_async_copy(nm_wide.at[j], nm_out.at[j], sems.at[3 + j]).wait()

    return pl.pallas_call(
        kernel,
        out_shape=(
            jax.ShapeDtypeStruct((mats, rows, dim), jnp.float32),
            jax.ShapeDtypeStruct((mats, rows, dim), jnp.bfloat16),
            jax.ShapeDtypeStruct((1, hid, dim), jnp.bfloat16),
        ),
        in_specs=[
            pl.BlockSpec(memory_space=pltpu.SMEM),
            pl.BlockSpec(memory_space=pl.ANY),
            pl.BlockSpec(memory_space=pl.ANY),
        ],
        out_specs=(pl.BlockSpec(memory_space=pl.ANY),) * 3,
        scratch_shapes=[
            pltpu.VMEM((mats, rows, dim), jnp.bfloat16),
            pltpu.VMEM((mats, rows, dim), jnp.float32),
            pltpu.VMEM((hid, dim), jnp.bfloat16),
            pltpu.SemaphoreType.DMA((3 + mats,)),
        ],
        cost_estimate=pl.CostEstimate(flops=0, bytes_accessed=16 * mats * rows * dim, transcendentals=0),
        compiler_params=pltpu.CompilerParams(vmem_limit_bytes=58 * 1024 * 1024),
    )


def solution(mesh):
    n_dp, n_zero = mesh.shape["dp"], mesh.shape["zero"]

    def kernel_step(grad_parts, momentum, owner_table):
        _, mats, rows, dim = grad_parts.shape
        nm, update = make_kernel(n_dp, n_zero, mats, rows, dim)(grad_parts, momentum)
        return make_finish(n_zero, mats, rows, dim)(owner_table, nm, update)

    def on_device(grad_parts, momentum, owner_table):
        _, mats, rows, dim = grad_parts.shape
        fits = (
            mats == 3
            and n_zero == 4
            and n_dp % 2 == 0
            and n_dp >= 4
            and dim % (LANES * n_dp) == 0
            and dim % 256 == 0
            and rows % 16 == 0
        )
        body = kernel_step if fits else general_step
        return body(grad_parts, momentum, owner_table)

    placed = (P("dp", None, "zero", None), P(None, "zero", None), P())
    return jax.shard_map(
        on_device,
        mesh=mesh,
        in_specs=placed,
        out_specs=(P(None, "zero", None), P(None, "zero", None), P("zero", None, None)),
        check_vma=False,
    )
```

```python
import math

import jax
import jax.numpy as jnp
from jax import lax
from jax.experimental import pallas as pl
from jax.experimental.pallas import tpu as pltpu
from jax.sharding import PartitionSpec as P

ITERS = 2
COEF_A = 3.4445
COEF_B = -4.775
COEF_C = 2.0315
MOMENTUM_DECAY = 0.95
NORM_EPSILON = 1e-07
MESH = pl.DeviceIdType.MESH
LANES = 128


def orthogonalize(matrix):
    current = matrix
    iterate = matrix.astype(jnp.float32)
    for step in range(ITERS):
        gram_matrix = jnp.dot(current, current.T, preferred_element_type=jnp.float32).astype(
            jnp.bfloat16
        )
        squared = jnp.dot(gram_matrix, gram_matrix, preferred_element_type=jnp.float32)
        poly_term = (COEF_B * gram_matrix.astype(jnp.float32) + COEF_C * squared).astype(
            jnp.bfloat16
        )
        iterate = COEF_A * current.astype(jnp.float32) + jnp.dot(
            poly_term, current, preferred_element_type=jnp.float32
        )
        if step + 1 < ITERS:
            current = iterate.astype(jnp.bfloat16)
    return (0.2 * math.sqrt(matrix.shape[1]) * iterate).astype(jnp.bfloat16)


def general_step(grad_parts, momentum, owner_table):
    my_index = lax.axis_index("zero")
    local_part = grad_parts[0].astype(jnp.float32)
    summed = lax.psum(local_part, "dp")
    new_momentum = MOMENTUM_DECAY * momentum + summed
    partial_value = jnp.sum(new_momentum * new_momentum, axis=(1, 2))
    squares = lax.psum(partial_value, "zero")
    inverse = 1.0 / (jnp.sqrt(squares) + NORM_EPSILON)
    start_rows = (new_momentum * inverse[:, None, None]).astype(jnp.bfloat16)
    mine_mask = (owner_table == my_index).astype(jnp.bfloat16)
    gathered = lax.all_gather(start_rows, "zero", axis=1, tiled=True)
    full_matrix = jnp.einsum(
        "j,jrd->rd", mine_mask, gathered, preferred_element_type=jnp.float32
    ).astype(jnp.bfloat16)
    result = orthogonalize(full_matrix)
    contrib = mine_mask.astype(jnp.float32)[:, None, None] * result.astype(jnp.float32)[None]
    update_rows = lax.psum_scatter(
        contrib.astype(jnp.bfloat16), "zero", scatter_dimension=1, tiled=True
    )
    return (new_momentum, update_rows, result[None])


def column_tiles(width, step=256):
    return [(at, min(step, width - at)) for at in range(0, width, step)]


def make_kernel(n_dp, n_zero, mats, rows, dim):
    hid = rows * n_zero
    half = hid // 2
    n_line = n_dp // 2
    width = dim // n_dp
    out_scale = 0.2 * math.sqrt(dim)

    def kernel(
        grad, momentum, nm_out, up_out,
        grads, stage, x, full, later, gram, parts, mom, poly, scale,
        rs_s, rs_r, s1_s, s1_r, s2_s, s2_r, s3_s, s3_r, s4_s, s4_r, gx_s, gx_r, xx_s, xx_r, local,
    ):
        d = lax.axis_index("dp")
        o = lax.axis_index("zero")
        zi, xi, yi, ci = d // 2, d % 2, o // 2, o % 2
        x_peer = zi * 2 + 1 - xi
        y_peer = (1 - yi) * 2 + ci
        c_peer = yi * 2 + 1 - ci

        def row(s):
            return pl.ds(pl.multiple_of(s * rows, 16), rows)

        def col(k):
            return pl.ds(pl.multiple_of(k * width, LANES), width)

        def chunk(j, s, k):
            return x.at[j, k, row(s), :]

        def line(r):
            return (zi + n_line - r) % n_line

        def remote(src, dst, send, recv, to):
            return pltpu.make_async_remote_copy(
                src_ref=src, dst_ref=dst, send_sem=send, recv_sem=recv,
                device_id=to, device_id_type=MESH,
            )

        def rs(j, r):
            p = (d + r) % n_dp
            return remote(stage.at[j, p], parts.at[j, r - 1], rs_s.at[j, r], rs_r.at[j, r], (p, o))

        def s1(j, r):
            c = chunk(j, o, d)
            return remote(c, c, s1_s.at[j, r], s1_r.at[j, r], (((zi + r) % n_line) * 2 + xi, o))

        def s1_in(j, r):
            c = chunk(j, o, line(r) * 2 + xi)
            return remote(c, c, s1_s.at[j, r], s1_r.at[j, r], (((zi + r) % n_line) * 2 + xi, o))

        def s2(j, r):
            c = chunk(j, o, line(r) * 2 + xi)
            return remote(c, c, s2_s.at[j, r], s2_r.at[j, r], (x_peer, o))

        def s2_in(j, r):
            c = chunk(j, o, line(r) * 2 + 1 - xi)
            return remote(c, c, s2_s.at[j, r], s2_r.at[j, r], (x_peer, o))

        def s3(j, r, h, s=None):
            k = line(r) * 2 + (xi if h == 0 else 1 - xi)
            c = chunk(j, o if s is None else s, k)
            return remote(c, c, s3_s.at[j, r, h], s3_r.at[j, r, h], (d, y_peer))

        def s3_in(j, r, h):
            return s3(j, r, h, y_peer)

        def s4(j, h, s=None):
            if s is None:
                s = o if h == 0 else y_peer
            c = x.at[j, :, row(s), :]
            return remote(c, c, s4_s.at[j, h], s4_r.at[j, h], (d, c_peer))

        def s4_in(j, h):
            return s4(j, h, c_peer if h == 0 else (1 - yi) * 2 + 1 - ci)

        def load_grad(j):
            return pltpu.make_async_copy(grad.at[0, j], grads.at[j], local.at[j])

        def own_momentum():
            return pltpu.make_async_copy(momentum.at[:, :, col(d)], mom, local.at[mats])

        def nm_copy(j):
            return pltpu.make_async_copy(full.at[j, row(o), :], nm_out.at[j], local.at[mats + 1 + j])

        def up_copy(j):
            return pltpu.make_async_copy(later.at[ITERS - 1, j], up_out.at[j], local.at[2 * mats + 1 + j])

        peers = [((d + r) % n_dp, o) for r in range(1, n_dp)] + [(d, y_peer), (d, c_peer)]
        barrier = pltpu.get_barrier_semaphore()
        for j in range(mats):
            load_grad(j).start()
        own_momentum().start()
        for to in peers:
            pl.semaphore_signal(barrier, inc=1, device_id=to, device_id_type=MESH)
        for j in range(mats):
            load_grad(j).wait()
            for k in range(n_dp):
                stage[j, k] = grads[j, :, k * width : (k + 1) * width]
        pl.semaphore_wait(barrier, len(peers))

        def send_parts(j):
            for r in range(1, n_dp):
                rs(j, r).start()

        def phase_a(j):
            if j == 0:
                own_momentum().wait()
            for r in range(1, n_dp):
                rs(j, r).wait_recv()
            total = stage[j, d].astype(jnp.float32)
            for r in range(n_dp - 1):
                total = total + parts[j, r].astype(jnp.float32)
            x[j, d, row(o), :] = (MOMENTUM_DECAY * mom[j] + total).astype(jnp.bfloat16)
            s3(j, 0, 0).start()
            s2(j, 0).start()
            for r in range(1, n_line):
                s1(j, r).start()

        def phase_b(j):
            for r in range(1, n_line):
                s1_in(j, r).wait_recv()
                s2(j, r).start()
                s3(j, r, 0).start()

        def phase_c(j):
            for r in range(n_line):
                s2_in(j, r).wait_recv()
                s3(j, r, 1).start()
            s4(j, 0).start()

        def phase_d(j):
            for r in range(n_line):
                for h in range(2):
                    s3_in(j, r, h).wait_recv()
            s4(j, 1).start()

        def phase_e(j):
            for h in range(2):
                s4_in(j, h).wait_recv()

        def half_rows(c):
            return pl.ds(pl.multiple_of(c * half, 16), half)

        def gx(j, it, c=None):
            g = gram.at[j, it, half_rows(ci if c is None else c), :]
            return remote(g, g, gx_s.at[j, it], gx_r.at[j, it], (d, c_peer))

        def xx(j, it, c=None):
            v = later.at[it, j, half_rows(ci if c is None else c), :]
            return remote(v, v, xx_s.at[j, it], xx_r.at[j, it], (d, c_peer))

        mine = half_rows(ci)

        def source(j, it):
            return full.at[j] if it == 0 else later.at[it - 1, j]

        def gram_op(j, it):
            src = source(j, it)
            if it == 0:
                acc = jnp.zeros((1, width), jnp.float32)
                for k in range(n_dp):
                    v = x[j, k]
                    full[j, :, k * width : (k + 1) * width] = v
                    w = v.astype(jnp.float32)
                    acc = acc + jnp.sum(w * w, axis=0, keepdims=True)
                nm_copy(j).start()
                total = jnp.sum(acc, axis=1, keepdims=True)
                scale[j] = jnp.broadcast_to(1.0 / (jnp.sqrt(total) + NORM_EPSILON), scale.shape[1:])
            else:
                xx(j, it - 1, 1 - ci).wait_recv()
            for at, size in column_tiles(hid):
                g = lax.dot_general(
                    src[mine, :], src[at : at + size, :], (((1,), (1,)), ((), ())),
                    preferred_element_type=jnp.float32,
                )
                if it == 0:
                    s = scale[j, 0:1, 0:1]
                    g = g * s * s
                gram[j, it, mine, at : at + size] = g.astype(jnp.bfloat16)
            gx(j, it).start()

        def apply_op(j, it):
            src = source(j, it)
            gx(j, it, 1 - ci).wait_recv()
            for at, size in column_tiles(hid):
                q = jnp.dot(
                    gram[j, it, mine, :], gram[j, it, :, at : at + size],
                    preferred_element_type=jnp.float32,
                )
                block = gram[j, it, mine, at : at + size].astype(jnp.float32)
                poly[:, at : at + size] = (COEF_B * block + COEF_C * q).astype(jnp.bfloat16)

            def apply(i, carry):
                cols = pl.ds(pl.multiple_of(i * 256, 256), 256)
                y = COEF_A * src[mine, cols].astype(jnp.float32) + jnp.dot(
                    poly[...], src[:, cols], preferred_element_type=jnp.float32
                )
                if it == 0:
                    y = y * scale[j, 0:1, 0:1]
                if it == ITERS - 1:
                    y = y * out_scale
                later[it, j, mine, cols] = y.astype(jnp.bfloat16)
                return carry

            lax.fori_loop(0, dim // 256, apply, 0)
            xx(j, it).start()

        def finish(j):
            xx(j, ITERS - 1, 1 - ci).wait_recv()
            up_copy(j).start()

        send_parts(0)
        for r in range(1, n_dp):
            rs(0, r).wait_send()
            rs(1, r).start()
        phase_a(0)
        phase_b(0)
        send_parts(2)
        phase_c(0)
        phase_a(1)
        phase_d(0)
        phase_b(1)
        phase_c(1)
        phase_e(0)
        gram_op(0, 0)
        phase_a(2)
        phase_b(2)
        apply_op(0, 0)
        gram_op(0, 1)
        phase_c(2)
        phase_d(1)
        phase_e(1)
        gram_op(1, 0)
        apply_op(0, 1)
        apply_op(1, 0)
        phase_d(2)
        phase_e(2)
        gram_op(2, 0)
        gram_op(1, 1)
        finish(0)
        apply_op(2, 0)
        apply_op(1, 1)
        gram_op(2, 1)
        finish(1)
        apply_op(2, 1)
        finish(2)

        for j in range(mats):
            if j > 0:
                for r in range(1, n_dp):
                    rs(j, r).wait_send()
            for r in range(1, n_line):
                s1(j, r).wait_send()
            for r in range(n_line):
                s2(j, r).wait_send()
                for h in range(2):
                    s3(j, r, h).wait_send()
            for h in range(2):
                s4(j, h).wait_send()
            for it in range(ITERS):
                gx(j, it).wait_send()
                xx(j, it).wait_send()
            nm_copy(j).wait()
            up_copy(j).wait()

    dma = pltpu.SemaphoreType.DMA
    flops = mats * ITERS * hid * hid * (2 * dim + hid)
    return pl.pallas_call(
        kernel,
        out_shape=(
            jax.ShapeDtypeStruct((mats, rows, dim), jnp.bfloat16),
            jax.ShapeDtypeStruct((mats, hid, dim), jnp.bfloat16),
        ),
        in_specs=[pl.BlockSpec(memory_space=pl.ANY)] * 2,
        out_specs=(pl.BlockSpec(memory_space=pl.ANY),) * 2,
        scratch_shapes=[
            pltpu.VMEM((mats, rows, dim), jnp.bfloat16),
            pltpu.VMEM((mats, n_dp, rows, width), jnp.bfloat16),
            pltpu.VMEM((mats, n_dp, hid, width), jnp.bfloat16),
            pltpu.VMEM((mats, hid, dim), jnp.bfloat16),
            pltpu.VMEM((ITERS, mats, hid, dim), jnp.bfloat16),
            pltpu.VMEM((mats, ITERS, hid, hid), jnp.bfloat16),
            pltpu.VMEM((mats, n_dp - 1, rows, width), jnp.bfloat16),
            pltpu.VMEM((mats, rows, width), jnp.float32),
            pltpu.VMEM((half, hid), jnp.bfloat16),
            pltpu.VMEM((mats, 8, LANES), jnp.float32),
            dma((mats, n_dp)), dma((mats, n_dp)),
            dma((mats, n_line)), dma((mats, n_line)),
            dma((mats, n_line)), dma((mats, n_line)),
            dma((mats, n_line, 2)), dma((mats, n_line, 2)),
            dma((mats, 2)), dma((mats, 2)),
            dma((mats, ITERS)), dma((mats, ITERS)),
            dma((mats, ITERS)), dma((mats, ITERS)),
            dma((3 * mats + 1,)),
        ],
        cost_estimate=pl.CostEstimate(flops=flops, bytes_accessed=16 * mats * rows * dim, transcendentals=0),
        compiler_params=pltpu.CompilerParams(
            collective_id=0, has_side_effects=True, vmem_limit_bytes=58 * 1024 * 1024
        ),
    )


def make_finish(n_zero, mats, rows, dim):
    hid = rows * n_zero

    def kernel(table, nm, update, nm_out, up_out, own_out, nm_in, nm_wide, up, own, sems):
        me = lax.axis_index("zero")
        rows_mine = update.at[:, pl.ds(pl.multiple_of(me * rows, 16), rows), :]
        nm_load = pltpu.make_async_copy(nm, nm_in, sems.at[0])
        nm_load.start()
        up_load = pltpu.make_async_copy(rows_mine, up, sems.at[1])
        up_load.start()
        count = jnp.int32(0)
        for j in range(mats):
            owned = table[j] == me
            count = count + owned.astype(jnp.int32)

            @pl.when(owned)
            def _():
                pltpu.make_async_copy(update.at[j], own, sems.at[2]).start()

        nm_load.wait()
        nm_store = []
        for j in range(mats):
            nm_wide[j] = nm_in[j].astype(jnp.float32)
            nm_store.append(pltpu.make_async_copy(nm_wide.at[j], nm_out.at[j], sems.at[5 + j]))
            nm_store[j].start()
        up_load.wait()
        up_store = pltpu.make_async_copy(up, up_out, sems.at[3])
        up_store.start()

        @pl.when(count == 0)
        def _():
            own[...] = jnp.zeros(own.shape, own.dtype)

        @pl.when(count > 0)
        def _():
            pltpu.make_async_copy(update.at[0], own, sems.at[2]).wait()

        own_store = pltpu.make_async_copy(own, own_out.at[0], sems.at[4])
        own_store.start()
        up_store.wait()
        own_store.wait()
        for j in range(mats):
            nm_store[j].wait()

    return pl.pallas_call(
        kernel,
        out_shape=(
            jax.ShapeDtypeStruct((mats, rows, dim), jnp.float32),
            jax.ShapeDtypeStruct((mats, rows, dim), jnp.bfloat16),
            jax.ShapeDtypeStruct((1, hid, dim), jnp.bfloat16),
        ),
        in_specs=[
            pl.BlockSpec(memory_space=pltpu.SMEM),
            pl.BlockSpec(memory_space=pl.ANY),
            pl.BlockSpec(memory_space=pl.ANY),
        ],
        out_specs=(pl.BlockSpec(memory_space=pl.ANY),) * 3,
        scratch_shapes=[
            pltpu.VMEM((mats, rows, dim), jnp.bfloat16),
            pltpu.VMEM((mats, rows, dim), jnp.float32),
            pltpu.VMEM((mats, rows, dim), jnp.bfloat16),
            pltpu.VMEM((hid, dim), jnp.bfloat16),
            pltpu.SemaphoreType.DMA((5 + mats,)),
        ],
        cost_estimate=pl.CostEstimate(flops=0, bytes_accessed=16 * mats * rows * dim, transcendentals=0),
        compiler_params=pltpu.CompilerParams(vmem_limit_bytes=58 * 1024 * 1024),
    )


def solution(mesh):
    n_dp, n_zero = mesh.shape["dp"], mesh.shape["zero"]

    def kernel_step(grad_parts, momentum, owner_table):
        _, mats, rows, dim = grad_parts.shape
        nm, update = make_kernel(n_dp, n_zero, mats, rows, dim)(grad_parts, momentum)
        return make_finish(n_zero, mats, rows, dim)(owner_table, nm, update)

    def on_device(grad_parts, momentum, owner_table):
        _, mats, rows, dim = grad_parts.shape
        fits = (
            mats == 3
            and n_zero == 4
            and n_dp % 2 == 0
            and n_dp >= 4
            and dim % (LANES * n_dp) == 0
            and dim % 256 == 0
            and rows % 16 == 0
        )
        body = kernel_step if fits else general_step
        return body(grad_parts, momentum, owner_table)

    placed = (P("dp", None, "zero", None), P(None, "zero", None), P())
    return jax.shard_map(
        on_device,
        mesh=mesh,
        in_specs=placed,
        out_specs=(P(None, "zero", None), P(None, "zero", None), P("zero", None, None)),
        check_vma=False,
    )
```

```python
import math

import jax
import jax.numpy as jnp
from jax import lax
from jax.experimental import pallas as pl
from jax.experimental.pallas import tpu as pltpu
from jax.sharding import PartitionSpec as P

ITERS = 2
COEF_A = 3.4445
COEF_B = -4.775
COEF_C = 2.0315
MOMENTUM_DECAY = 0.95
NORM_EPSILON = 1e-07
MESH = pl.DeviceIdType.MESH
LANES = 128


def orthogonalize(matrix):
    current = matrix
    iterate = matrix.astype(jnp.float32)
    for step in range(ITERS):
        gram_matrix = jnp.dot(current, current.T, preferred_element_type=jnp.float32).astype(
            jnp.bfloat16
        )
        squared = jnp.dot(gram_matrix, gram_matrix, preferred_element_type=jnp.float32)
        poly_term = (COEF_B * gram_matrix.astype(jnp.float32) + COEF_C * squared).astype(
            jnp.bfloat16
        )
        iterate = COEF_A * current.astype(jnp.float32) + jnp.dot(
            poly_term, current, preferred_element_type=jnp.float32
        )
        if step + 1 < ITERS:
            current = iterate.astype(jnp.bfloat16)
    return (0.2 * math.sqrt(matrix.shape[1]) * iterate).astype(jnp.bfloat16)


def general_step(grad_parts, momentum, owner_table):
    my_index = lax.axis_index("zero")
    local_part = grad_parts[0].astype(jnp.float32)
    summed = lax.psum(local_part, "dp")
    new_momentum = MOMENTUM_DECAY * momentum + summed
    partial_value = jnp.sum(new_momentum * new_momentum, axis=(1, 2))
    squares = lax.psum(partial_value, "zero")
    inverse = 1.0 / (jnp.sqrt(squares) + NORM_EPSILON)
    start_rows = (new_momentum * inverse[:, None, None]).astype(jnp.bfloat16)
    mine_mask = (owner_table == my_index).astype(jnp.bfloat16)
    gathered = lax.all_gather(start_rows, "zero", axis=1, tiled=True)
    full_matrix = jnp.einsum(
        "j,jrd->rd", mine_mask, gathered, preferred_element_type=jnp.float32
    ).astype(jnp.bfloat16)
    result = orthogonalize(full_matrix)
    contrib = mine_mask.astype(jnp.float32)[:, None, None] * result.astype(jnp.float32)[None]
    update_rows = lax.psum_scatter(
        contrib.astype(jnp.bfloat16), "zero", scatter_dimension=1, tiled=True
    )
    return (new_momentum, update_rows, result[None])


def column_tiles(width, step=256):
    return [(at, min(step, width - at)) for at in range(0, width, step)]


def make_kernel(n_dp, n_zero, mats, rows, dim):
    hid = rows * n_zero
    half = hid // 2
    n_line = n_dp // 2
    width = dim // n_dp
    out_scale = 0.2 * math.sqrt(dim)

    def kernel(
        grad, momentum, nm_out, up_out,
        grads, stage, pairs_in, pairs, x, full, later, gram, parts, mom, poly, scale,
        ra_s, ra_r, rs_s, rs_r, s1_s, s1_r, s2_s, s2_r, s3_s, s3_r, s4_s, s4_r, gx_s, gx_r, xx_s, xx_r, local,
    ):
        d = lax.axis_index("dp")
        o = lax.axis_index("zero")
        zi, xi, yi, ci = d // 2, d % 2, o // 2, o % 2
        x_peer = zi * 2 + 1 - xi
        y_peer = (1 - yi) * 2 + ci
        c_peer = yi * 2 + 1 - ci

        def row(s):
            return pl.ds(pl.multiple_of(s * rows, 16), rows)

        def col(k):
            return pl.ds(pl.multiple_of(k * width, LANES), width)

        def chunk(j, s, k):
            return x.at[j, k, row(s), :]

        def line(r):
            return (zi + n_line - r) % n_line

        def remote(src, dst, send, recv, to):
            return pltpu.make_async_remote_copy(
                src_ref=src, dst_ref=dst, send_sem=send, recv_sem=recv,
                device_id=to, device_id_type=MESH,
            )

        def ra(j, r):
            k = ((zi + r) % n_line) * 2 + 1 - xi
            return remote(stage.at[j, k], pairs_in.at[j, r], ra_s.at[j, r], ra_r.at[j, r], (x_peer, o))

        def rb(j, r):
            to = (((zi + r) % n_line) * 2 + xi, o)
            return remote(pairs.at[j, r - 1], parts.at[j, r - 1], rs_s.at[j, r], rs_r.at[j, r], to)

        def s1(j, r):
            c = chunk(j, o, d)
            return remote(c, c, s1_s.at[j, r], s1_r.at[j, r], (((zi + r) % n_line) * 2 + xi, o))

        def s1_in(j, r):
            c = chunk(j, o, line(r) * 2 + xi)
            return remote(c, c, s1_s.at[j, r], s1_r.at[j, r], (((zi + r) % n_line) * 2 + xi, o))

        def s2(j, r):
            c = chunk(j, o, line(r) * 2 + xi)
            return remote(c, c, s2_s.at[j, r], s2_r.at[j, r], (x_peer, o))

        def s2_in(j, r):
            c = chunk(j, o, line(r) * 2 + 1 - xi)
            return remote(c, c, s2_s.at[j, r], s2_r.at[j, r], (x_peer, o))

        def s3(j, r, h, s=None):
            k = line(r) * 2 + (xi if h == 0 else 1 - xi)
            c = chunk(j, o if s is None else s, k)
            return remote(c, c, s3_s.at[j, r, h], s3_r.at[j, r, h], (d, y_peer))

        def s3_in(j, r, h):
            return s3(j, r, h, y_peer)

        def s4(j, h, s=None):
            if s is None:
                s = o if h == 0 else y_peer
            c = x.at[j, :, row(s), :]
            return remote(c, c, s4_s.at[j, h], s4_r.at[j, h], (d, c_peer))

        def s4_in(j, h):
            return s4(j, h, c_peer if h == 0 else (1 - yi) * 2 + 1 - ci)

        def load_grad(j):
            return pltpu.make_async_copy(grad.at[0, j], grads.at[j], local.at[j])

        def own_momentum():
            return pltpu.make_async_copy(momentum.at[:, :, col(d)], mom, local.at[mats])

        def nm_copy(j):
            return pltpu.make_async_copy(full.at[j, row(o), :], nm_out.at[j], local.at[mats + 1 + j])

        def up_copy(j):
            return pltpu.make_async_copy(later.at[ITERS - 1, j], up_out.at[j], local.at[2 * mats + 1 + j])

        peers = [(((zi + r) % n_line) * 2 + xi, o) for r in range(1, n_line)]
        peers += [(x_peer, o), (d, y_peer), (d, c_peer)]
        barrier = pltpu.get_barrier_semaphore()
        for j in range(mats):
            load_grad(j).start()
        own_momentum().start()
        for to in peers:
            pl.semaphore_signal(barrier, inc=1, device_id=to, device_id_type=MESH)
        for j in range(mats):
            load_grad(j).wait()
            for k in range(n_dp):
                stage[j, k] = grads[j, :, k * width : (k + 1) * width]
        pl.semaphore_wait(barrier, len(peers))

        def send_parts(j):
            for r in [*range(1, n_line), 0]:
                ra(j, r).start()

        def pair(j, r):
            k = ((zi + r) % n_line) * 2 + xi
            return stage[j, k].astype(jnp.float32) + pairs_in[j, r].astype(jnp.float32)

        def phase_p(j):
            for r in range(1, n_line):
                ra(j, r).wait_recv()
                pairs[j, r - 1] = pair(j, r).astype(jnp.bfloat16)
                rb(j, r).start()

        def phase_a(j):
            if j == 0:
                own_momentum().wait()
            ra(j, 0).wait_recv()
            for r in range(1, n_line):
                rb(j, r).wait_recv()
            total = pair(j, 0)
            for r in range(n_line - 1):
                total = total + parts[j, r].astype(jnp.float32)
            x[j, d, row(o), :] = (MOMENTUM_DECAY * mom[j] + total).astype(jnp.bfloat16)
            s3(j, 0, 0).start()
            s2(j, 0).start()
            for r in range(1, n_line):
                s1(j, r).start()

        def phase_b(j):
            for r in range(1, n_line):
                s1_in(j, r).wait_recv()
                s2(j, r).start()
                s3(j, r, 0).start()

        def phase_c(j):
            for r in range(n_line):
                s2_in(j, r).wait_recv()
                s3(j, r, 1).start()
            s4(j, 0).start()

        def phase_d(j):
            for r in range(n_line):
                for h in range(2):
                    s3_in(j, r, h).wait_recv()
            s4(j, 1).start()

        def phase_e(j):
            for h in range(2):
                s4_in(j, h).wait_recv()

        def half_rows(c):
            return pl.ds(pl.multiple_of(c * half, 16), half)

        def gx(j, it, c=None):
            g = gram.at[j, it, half_rows(ci if c is None else c), :]
            return remote(g, g, gx_s.at[j, it], gx_r.at[j, it], (d, c_peer))

        def xx(j, it, c=None):
            v = later.at[it, j, half_rows(ci if c is None else c), :]
            return remote(v, v, xx_s.at[j, it], xx_r.at[j, it], (d, c_peer))

        mine = half_rows(ci)

        def source(j, it):
            return full.at[j] if it == 0 else later.at[it - 1, j]

        def gram_op(j, it):
            src = source(j, it)
            if it == 0:
                acc = jnp.zeros((1, width), jnp.float32)
                for k in range(n_dp):
                    v = x[j, k]
                    full[j, :, k * width : (k + 1) * width] = v
                    w = v.astype(jnp.float32)
                    acc = acc + jnp.sum(w * w, axis=0, keepdims=True)
                nm_copy(j).start()
                total = jnp.sum(acc, axis=1, keepdims=True)
                scale[j] = jnp.broadcast_to(1.0 / (jnp.sqrt(total) + NORM_EPSILON), scale.shape[1:])
            else:
                xx(j, it - 1, 1 - ci).wait_recv()
            for at, size in column_tiles(hid):
                g = lax.dot_general(
                    src[mine, :], src[at : at + size, :], (((1,), (1,)), ((), ())),
                    preferred_element_type=jnp.float32,
                )
                if it == 0:
                    s = scale[j, 0:1, 0:1]
                    g = g * s * s
                gram[j, it, mine, at : at + size] = g.astype(jnp.bfloat16)
            gx(j, it).start()

        def apply_op(j, it):
            src = source(j, it)
            gx(j, it, 1 - ci).wait_recv()
            for at, size in column_tiles(hid):
                q = jnp.dot(
                    gram[j, it, mine, :], gram[j, it, :, at : at + size],
                    preferred_element_type=jnp.float32,
                )
                block = gram[j, it, mine, at : at + size].astype(jnp.float32)
                poly[:, at : at + size] = (COEF_B * block + COEF_C * q).astype(jnp.bfloat16)

            def apply(i, carry):
                cols = pl.ds(pl.multiple_of(i * 256, 256), 256)
                y = COEF_A * src[mine, cols].astype(jnp.float32) + jnp.dot(
                    poly[...], src[:, cols], preferred_element_type=jnp.float32
                )
                if it == 0:
                    y = y * scale[j, 0:1, 0:1]
                if it == ITERS - 1:
                    y = y * out_scale
                later[it, j, mine, cols] = y.astype(jnp.bfloat16)
                return carry

            lax.fori_loop(0, dim // 256, apply, 0)
            xx(j, it).start()

        def finish(j):
            xx(j, ITERS - 1, 1 - ci).wait_recv()
            up_copy(j).start()

        send_parts(0)
        send_parts(1)
        phase_p(0)
        send_parts(2)
        phase_p(1)
        phase_a(0)
        phase_b(0)
        phase_p(2)
        phase_c(0)
        phase_a(1)
        phase_d(0)
        phase_b(1)
        phase_c(1)
        phase_e(0)
        gram_op(0, 0)
        phase_a(2)
        phase_b(2)
        apply_op(0, 0)
        gram_op(0, 1)
        phase_c(2)
        phase_d(1)
        phase_e(1)
        gram_op(1, 0)
        apply_op(0, 1)
        apply_op(1, 0)
        phase_d(2)
        phase_e(2)
        gram_op(2, 0)
        gram_op(1, 1)
        finish(0)
        apply_op(2, 0)
        apply_op(1, 1)
        gram_op(2, 1)
        finish(1)
        apply_op(2, 1)
        finish(2)

        for j in range(mats):
            for r in range(n_line):
                ra(j, r).wait_send()
            for r in range(1, n_line):
                rb(j, r).wait_send()
                s1(j, r).wait_send()
            for r in range(n_line):
                s2(j, r).wait_send()
                for h in range(2):
                    s3(j, r, h).wait_send()
            for h in range(2):
                s4(j, h).wait_send()
            for it in range(ITERS):
                gx(j, it).wait_send()
                xx(j, it).wait_send()
            nm_copy(j).wait()
            up_copy(j).wait()

    dma = pltpu.SemaphoreType.DMA
    flops = mats * ITERS * hid * hid * (2 * dim + hid)
    return pl.pallas_call(
        kernel,
        out_shape=(
            jax.ShapeDtypeStruct((mats, rows, dim), jnp.bfloat16),
            jax.ShapeDtypeStruct((mats, hid, dim), jnp.bfloat16),
        ),
        in_specs=[pl.BlockSpec(memory_space=pl.ANY)] * 2,
        out_specs=(pl.BlockSpec(memory_space=pl.ANY),) * 2,
        scratch_shapes=[
            pltpu.VMEM((mats, rows, dim), jnp.bfloat16),
            pltpu.VMEM((mats, n_dp, rows, width), jnp.bfloat16),
            pltpu.VMEM((mats, n_line, rows, width), jnp.bfloat16),
            pltpu.VMEM((mats, n_line - 1, rows, width), jnp.bfloat16),
            pltpu.VMEM((mats, n_dp, hid, width), jnp.bfloat16),
            pltpu.VMEM((mats, hid, dim), jnp.bfloat16),
            pltpu.VMEM((ITERS, mats, hid, dim), jnp.bfloat16),
            pltpu.VMEM((mats, ITERS, hid, hid), jnp.bfloat16),
            pltpu.VMEM((mats, n_line - 1, rows, width), jnp.bfloat16),
            pltpu.VMEM((mats, rows, width), jnp.float32),
            pltpu.VMEM((half, hid), jnp.bfloat16),
            pltpu.VMEM((mats, 8, LANES), jnp.float32),
            dma((mats, n_line)), dma((mats, n_line)),
            dma((mats, n_line)), dma((mats, n_line)),
            dma((mats, n_line)), dma((mats, n_line)),
            dma((mats, n_line)), dma((mats, n_line)),
            dma((mats, n_line, 2)), dma((mats, n_line, 2)),
            dma((mats, 2)), dma((mats, 2)),
            dma((mats, ITERS)), dma((mats, ITERS)),
            dma((mats, ITERS)), dma((mats, ITERS)),
            dma((3 * mats + 1,)),
        ],
        cost_estimate=pl.CostEstimate(flops=flops, bytes_accessed=16 * mats * rows * dim, transcendentals=0),
        compiler_params=pltpu.CompilerParams(
            collective_id=0, has_side_effects=True, vmem_limit_bytes=58 * 1024 * 1024
        ),
    )


def make_finish(n_zero, mats, rows, dim):
    hid = rows * n_zero

    def kernel(table, nm, update, nm_out, up_out, own_out, nm_in, nm_wide, up, own, sems):
        me = lax.axis_index("zero")
        rows_mine = update.at[:, pl.ds(pl.multiple_of(me * rows, 16), rows), :]
        nm_load = pltpu.make_async_copy(nm, nm_in, sems.at[0])
        nm_load.start()
        up_load = pltpu.make_async_copy(rows_mine, up, sems.at[1])
        up_load.start()
        count = jnp.int32(0)
        for j in range(mats):
            owned = table[j] == me
            count = count + owned.astype(jnp.int32)

            @pl.when(owned)
            def _():
                pltpu.make_async_copy(update.at[j], own, sems.at[2]).start()

        nm_load.wait()
        nm_store = []
        for j in range(mats):
            nm_wide[j] = nm_in[j].astype(jnp.float32)
            nm_store.append(pltpu.make_async_copy(nm_wide.at[j], nm_out.at[j], sems.at[5 + j]))
            nm_store[j].start()
        up_load.wait()
        up_store = pltpu.make_async_copy(up, up_out, sems.at[3])
        up_store.start()

        @pl.when(count == 0)
        def _():
            own[...] = jnp.zeros(own.shape, own.dtype)

        @pl.when(count > 0)
        def _():
            pltpu.make_async_copy(update.at[0], own, sems.at[2]).wait()

        own_store = pltpu.make_async_copy(own, own_out.at[0], sems.at[4])
        own_store.start()
        up_store.wait()
        own_store.wait()
        for j in range(mats):
            nm_store[j].wait()

    return pl.pallas_call(
        kernel,
        out_shape=(
            jax.ShapeDtypeStruct((mats, rows, dim), jnp.float32),
            jax.ShapeDtypeStruct((mats, rows, dim), jnp.bfloat16),
            jax.ShapeDtypeStruct((1, hid, dim), jnp.bfloat16),
        ),
        in_specs=[
            pl.BlockSpec(memory_space=pltpu.SMEM),
            pl.BlockSpec(memory_space=pl.ANY),
            pl.BlockSpec(memory_space=pl.ANY),
        ],
        out_specs=(pl.BlockSpec(memory_space=pl.ANY),) * 3,
        scratch_shapes=[
            pltpu.VMEM((mats, rows, dim), jnp.bfloat16),
            pltpu.VMEM((mats, rows, dim), jnp.float32),
            pltpu.VMEM((mats, rows, dim), jnp.bfloat16),
            pltpu.VMEM((hid, dim), jnp.bfloat16),
            pltpu.SemaphoreType.DMA((5 + mats,)),
        ],
        cost_estimate=pl.CostEstimate(flops=0, bytes_accessed=16 * mats * rows * dim, transcendentals=0),
        compiler_params=pltpu.CompilerParams(vmem_limit_bytes=58 * 1024 * 1024),
    )


def solution(mesh):
    n_dp, n_zero = mesh.shape["dp"], mesh.shape["zero"]

    def kernel_step(grad_parts, momentum, owner_table):
        _, mats, rows, dim = grad_parts.shape
        nm, update = make_kernel(n_dp, n_zero, mats, rows, dim)(grad_parts, momentum)
        return make_finish(n_zero, mats, rows, dim)(owner_table, nm, update)

    def on_device(grad_parts, momentum, owner_table):
        _, mats, rows, dim = grad_parts.shape
        fits = (
            mats == 3
            and n_zero == 4
            and n_dp % 2 == 0
            and n_dp >= 4
            and dim % (LANES * n_dp) == 0
            and dim % 256 == 0
            and rows % 16 == 0
        )
        body = kernel_step if fits else general_step
        return body(grad_parts, momentum, owner_table)

    placed = (P("dp", None, "zero", None), P(None, "zero", None), P())
    return jax.shard_map(
        on_device,
        mesh=mesh,
        in_specs=placed,
        out_specs=(P(None, "zero", None), P(None, "zero", None), P("zero", None, None)),
        check_vma=False,
    )
```

```python
import math

import jax
import jax.numpy as jnp
from jax import lax
from jax.experimental import pallas as pl
from jax.experimental.pallas import tpu as pltpu
from jax.sharding import PartitionSpec as P

ITERS = 2
COEF_A = 3.4445
COEF_B = -4.775
COEF_C = 2.0315
MOMENTUM_DECAY = 0.95
NORM_EPSILON = 1e-07
MESH = pl.DeviceIdType.MESH
LANES = 128


def orthogonalize(matrix):
    current = matrix
    iterate = matrix.astype(jnp.float32)
    for step in range(ITERS):
        gram_matrix = jnp.dot(current, current.T, preferred_element_type=jnp.float32).astype(
            jnp.bfloat16
        )
        squared = jnp.dot(gram_matrix, gram_matrix, preferred_element_type=jnp.float32)
        poly_term = (COEF_B * gram_matrix.astype(jnp.float32) + COEF_C * squared).astype(
            jnp.bfloat16
        )
        iterate = COEF_A * current.astype(jnp.float32) + jnp.dot(
            poly_term, current, preferred_element_type=jnp.float32
        )
        if step + 1 < ITERS:
            current = iterate.astype(jnp.bfloat16)
    return (0.2 * math.sqrt(matrix.shape[1]) * iterate).astype(jnp.bfloat16)


def general_step(grad_parts, momentum, owner_table):
    my_index = lax.axis_index("zero")
    local_part = grad_parts[0].astype(jnp.float32)
    summed = lax.psum(local_part, "dp")
    new_momentum = MOMENTUM_DECAY * momentum + summed
    partial_value = jnp.sum(new_momentum * new_momentum, axis=(1, 2))
    squares = lax.psum(partial_value, "zero")
    inverse = 1.0 / (jnp.sqrt(squares) + NORM_EPSILON)
    start_rows = (new_momentum * inverse[:, None, None]).astype(jnp.bfloat16)
    mine_mask = (owner_table == my_index).astype(jnp.bfloat16)
    gathered = lax.all_gather(start_rows, "zero", axis=1, tiled=True)
    full_matrix = jnp.einsum(
        "j,jrd->rd", mine_mask, gathered, preferred_element_type=jnp.float32
    ).astype(jnp.bfloat16)
    result = orthogonalize(full_matrix)
    contrib = mine_mask.astype(jnp.float32)[:, None, None] * result.astype(jnp.float32)[None]
    update_rows = lax.psum_scatter(
        contrib.astype(jnp.bfloat16), "zero", scatter_dimension=1, tiled=True
    )
    return (new_momentum, update_rows, result[None])


def column_tiles(width, step=256):
    return [(at, min(step, width - at)) for at in range(0, width, step)]


def make_kernel(n_dp, n_zero, mats, rows, dim):
    hid = rows * n_zero
    half = hid // 2
    gram_tiles = len(column_tiles(hid))
    n_line = n_dp // 2
    width = dim // n_dp
    out_scale = 0.2 * math.sqrt(dim)

    def kernel(
        grad, momentum, nm_out, up_out,
        grads, stage, pairs_in, pairs, x, full, later, gram, parts, mom, poly, scale,
        ra_s, ra_r, rs_s, rs_r, s1_s, s1_r, s2_s, s2_r, s3_s, s3_r, s4_s, s4_r, gx_s, gx_r, xx_s, xx_r, local,
    ):
        d = lax.axis_index("dp")
        o = lax.axis_index("zero")
        zi, xi, yi, ci = d // 2, d % 2, o // 2, o % 2
        x_peer = zi * 2 + 1 - xi
        y_peer = (1 - yi) * 2 + ci
        c_peer = yi * 2 + 1 - ci

        def row(s):
            return pl.ds(pl.multiple_of(s * rows, 16), rows)

        def col(k):
            return pl.ds(pl.multiple_of(k * width, LANES), width)

        def chunk(j, s, k):
            return x.at[j, k, row(s), :]

        def line(r):
            return (zi + n_line - r) % n_line

        def remote(src, dst, send, recv, to):
            return pltpu.make_async_remote_copy(
                src_ref=src, dst_ref=dst, send_sem=send, recv_sem=recv,
                device_id=to, device_id_type=MESH,
            )

        def ra(j, r):
            k = ((zi + r) % n_line) * 2 + 1 - xi
            return remote(stage.at[j, k], pairs_in.at[j, r], ra_s.at[j, r], ra_r.at[j, r], (x_peer, o))

        def rb(j, r):
            to = (((zi + r) % n_line) * 2 + xi, o)
            return remote(pairs.at[j, r - 1], parts.at[j, r - 1], rs_s.at[j, r], rs_r.at[j, r], to)

        def s1(j, r):
            c = chunk(j, o, d)
            return remote(c, c, s1_s.at[j, r], s1_r.at[j, r], (((zi + r) % n_line) * 2 + xi, o))

        def s1_in(j, r):
            c = chunk(j, o, line(r) * 2 + xi)
            return remote(c, c, s1_s.at[j, r], s1_r.at[j, r], (((zi + r) % n_line) * 2 + xi, o))

        def s2(j, r):
            c = chunk(j, o, line(r) * 2 + xi)
            return remote(c, c, s2_s.at[j, r], s2_r.at[j, r], (x_peer, o))

        def s2_in(j, r):
            c = chunk(j, o, line(r) * 2 + 1 - xi)
            return remote(c, c, s2_s.at[j, r], s2_r.at[j, r], (x_peer, o))

        def s3(j, r, h, s=None):
            k = line(r) * 2 + (xi if h == 0 else 1 - xi)
            c = chunk(j, o if s is None else s, k)
            return remote(c, c, s3_s.at[j, r, h], s3_r.at[j, r, h], (d, y_peer))

        def s3_in(j, r, h):
            return s3(j, r, h, y_peer)

        def s4(j, h, s=None):
            if s is None:
                s = o if h == 0 else y_peer
            c = x.at[j, :, row(s), :]
            return remote(c, c, s4_s.at[j, h], s4_r.at[j, h], (d, c_peer))

        def s4_in(j, h):
            return s4(j, h, c_peer if h == 0 else (1 - yi) * 2 + 1 - ci)

        def load_grad(j):
            return pltpu.make_async_copy(grad.at[0, j], grads.at[j], local.at[j])

        def own_momentum():
            return pltpu.make_async_copy(momentum.at[:, :, col(d)], mom, local.at[mats])

        def nm_copy(j):
            return pltpu.make_async_copy(full.at[j, row(o), :], nm_out.at[j], local.at[mats + 1 + j])

        def up_copy(j):
            return pltpu.make_async_copy(later.at[ITERS - 1, j], up_out.at[j], local.at[2 * mats + 1 + j])

        peers = [(((zi + r) % n_line) * 2 + xi, o) for r in range(1, n_line)]
        peers += [(x_peer, o), (d, y_peer), (d, c_peer)]
        barrier = pltpu.get_barrier_semaphore()
        for j in range(mats):
            load_grad(j).start()
        own_momentum().start()
        for to in peers:
            pl.semaphore_signal(barrier, inc=1, device_id=to, device_id_type=MESH)

        def put_together(j):
            load_grad(j).wait()
            for k in range(n_dp):
                stage[j, k] = grads[j, :, k * width : (k + 1) * width]

        def send_parts(j):
            for r in [*range(1, n_line), 0]:
                ra(j, r).start()

        def pair(j, r):
            k = ((zi + r) % n_line) * 2 + xi
            return stage[j, k].astype(jnp.float32) + pairs_in[j, r].astype(jnp.float32)

        def phase_p(j):
            for r in range(1, n_line):
                ra(j, r).wait_recv()
                pairs[j, r - 1] = pair(j, r).astype(jnp.bfloat16)
                rb(j, r).start()

        def phase_a(j):
            if j == 0:
                own_momentum().wait()
            ra(j, 0).wait_recv()
            for r in range(1, n_line):
                rb(j, r).wait_recv()
            total = pair(j, 0)
            for r in range(n_line - 1):
                total = total + parts[j, r].astype(jnp.float32)
            x[j, d, row(o), :] = (MOMENTUM_DECAY * mom[j] + total).astype(jnp.bfloat16)
            s3(j, 0, 0).start()
            s2(j, 0).start()
            for r in range(1, n_line):
                s1(j, r).start()

        def phase_b(j):
            for r in range(1, n_line):
                s1_in(j, r).wait_recv()
                s2(j, r).start()
                s3(j, r, 0).start()

        def phase_c(j):
            for r in range(n_line):
                s2_in(j, r).wait_recv()
                s3(j, r, 1).start()
            s4(j, 0).start()

        def phase_d(j):
            for r in range(n_line):
                for h in range(2):
                    s3_in(j, r, h).wait_recv()
            s4(j, 1).start()

        def phase_e(j):
            for h in range(2):
                s4_in(j, h).wait_recv()

        def half_rows(c):
            return pl.ds(pl.multiple_of(c * half, 16), half)

        def gx(j, it, n, c=None):
            at, size = column_tiles(hid)[n]
            g = gram.at[j, it, half_rows(ci if c is None else c), at : at + size]
            return remote(g, g, gx_s.at[j, it, n], gx_r.at[j, it, n], (d, c_peer))

        def xx(j, it, n, c=None):
            cols = pl.ds(pl.multiple_of(n * 256, 256), 256)
            v = later.at[it, j, half_rows(ci if c is None else c), cols]
            return remote(v, v, xx_s.at[j, it, n], xx_r.at[j, it, n], (d, c_peer))

        def gx_wait(j, it):
            for n in range(gram_tiles):
                gx(j, it, n, 1 - ci).wait_recv()

        def xx_wait(j, it):
            for n in range(dim // 256):
                xx(j, it, n, 1 - ci).wait_recv()

        mine = half_rows(ci)

        def source(j, it):
            return full.at[j] if it == 0 else later.at[it - 1, j]

        def gram_op(j, it):
            src = source(j, it)
            if it == 0:
                acc = jnp.zeros((1, width), jnp.float32)
                for k in range(n_dp):
                    v = x[j, k]
                    full[j, :, k * width : (k + 1) * width] = v
                    w = v.astype(jnp.float32)
                    acc = acc + jnp.sum(w * w, axis=0, keepdims=True)
                nm_copy(j).start()
                total = jnp.sum(acc, axis=1, keepdims=True)
                scale[j] = jnp.broadcast_to(1.0 / (jnp.sqrt(total) + NORM_EPSILON), scale.shape[1:])
            else:
                xx_wait(j, it - 1)
            for n, (at, size) in enumerate(column_tiles(hid)):
                g = lax.dot_general(
                    src[mine, :], src[at : at + size, :], (((1,), (1,)), ((), ())),
                    preferred_element_type=jnp.float32,
                )
                if it == 0:
                    s = scale[j, 0:1, 0:1]
                    g = g * s * s
                gram[j, it, mine, at : at + size] = g.astype(jnp.bfloat16)
                gx(j, it, n).start()

        def apply_op(j, it):
            src = source(j, it)
            gx_wait(j, it)
            for at, size in column_tiles(hid):
                q = jnp.dot(
                    gram[j, it, mine, :], gram[j, it, :, at : at + size],
                    preferred_element_type=jnp.float32,
                )
                block = gram[j, it, mine, at : at + size].astype(jnp.float32)
                poly[:, at : at + size] = (COEF_B * block + COEF_C * q).astype(jnp.bfloat16)

            def apply(i, carry):
                cols = pl.ds(pl.multiple_of(i * 256, 256), 256)
                y = COEF_A * src[mine, cols].astype(jnp.float32) + jnp.dot(
                    poly[...], src[:, cols], preferred_element_type=jnp.float32
                )
                if it == 0:
                    y = y * scale[j, 0:1, 0:1]
                if it == ITERS - 1:
                    y = y * out_scale
                later[it, j, mine, cols] = y.astype(jnp.bfloat16)
                xx(j, it, i).start()
                return carry

            lax.fori_loop(0, dim // 256, apply, 0)

        def finish(j):
            xx_wait(j, ITERS - 1)
            up_copy(j).start()

        put_together(0)
        pl.semaphore_wait(barrier, len(peers))
        for j in range(mats):
            if j > 0:
                put_together(j)
            send_parts(j)
        phase_p(0)
        phase_p(1)
        phase_a(0)
        phase_p(2)
        phase_a(1)
        phase_b(0)
        phase_c(0)
        phase_a(2)
        phase_b(1)
        phase_d(0)
        phase_c(1)
        phase_b(2)
        phase_e(0)
        gram_op(0, 0)
        phase_c(2)
        phase_d(1)
        apply_op(0, 0)
        phase_e(1)
        gram_op(1, 0)
        phase_d(2)
        gram_op(0, 1)
        apply_op(1, 0)
        phase_e(2)
        gram_op(2, 0)
        apply_op(0, 1)
        gram_op(1, 1)
        apply_op(2, 0)
        finish(0)
        apply_op(1, 1)
        gram_op(2, 1)
        finish(1)
        apply_op(2, 1)
        finish(2)

        for j in range(mats):
            for r in range(n_line):
                ra(j, r).wait_send()
            for r in range(1, n_line):
                rb(j, r).wait_send()
                s1(j, r).wait_send()
            for r in range(n_line):
                s2(j, r).wait_send()
                for h in range(2):
                    s3(j, r, h).wait_send()
            for h in range(2):
                s4(j, h).wait_send()
            for it in range(ITERS):
                for n in range(gram_tiles):
                    gx(j, it, n).wait_send()
                for n in range(dim // 256):
                    xx(j, it, n).wait_send()
            nm_copy(j).wait()
            up_copy(j).wait()

    dma = pltpu.SemaphoreType.DMA
    flops = mats * ITERS * hid * hid * (2 * dim + hid)
    return pl.pallas_call(
        kernel,
        out_shape=(
            jax.ShapeDtypeStruct((mats, rows, dim), jnp.bfloat16),
            jax.ShapeDtypeStruct((mats, hid, dim), jnp.bfloat16),
        ),
        in_specs=[pl.BlockSpec(memory_space=pl.ANY)] * 2,
        out_specs=(pl.BlockSpec(memory_space=pl.ANY),) * 2,
        scratch_shapes=[
            pltpu.VMEM((mats, rows, dim), jnp.bfloat16),
            pltpu.VMEM((mats, n_dp, rows, width), jnp.bfloat16),
            pltpu.VMEM((mats, n_line, rows, width), jnp.bfloat16),
            pltpu.VMEM((mats, n_line - 1, rows, width), jnp.bfloat16),
            pltpu.VMEM((mats, n_dp, hid, width), jnp.bfloat16),
            pltpu.VMEM((mats, hid, dim), jnp.bfloat16),
            pltpu.VMEM((ITERS, mats, hid, dim), jnp.bfloat16),
            pltpu.VMEM((mats, ITERS, hid, hid), jnp.bfloat16),
            pltpu.VMEM((mats, n_line - 1, rows, width), jnp.bfloat16),
            pltpu.VMEM((mats, rows, width), jnp.float32),
            pltpu.VMEM((half, hid), jnp.bfloat16),
            pltpu.VMEM((mats, 8, LANES), jnp.float32),
            dma((mats, n_line)), dma((mats, n_line)),
            dma((mats, n_line)), dma((mats, n_line)),
            dma((mats, n_line)), dma((mats, n_line)),
            dma((mats, n_line)), dma((mats, n_line)),
            dma((mats, n_line, 2)), dma((mats, n_line, 2)),
            dma((mats, 2)), dma((mats, 2)),
            dma((mats, ITERS, gram_tiles)), dma((mats, ITERS, gram_tiles)),
            dma((mats, ITERS, dim // 256)), dma((mats, ITERS, dim // 256)),
            dma((3 * mats + 1,)),
        ],
        cost_estimate=pl.CostEstimate(flops=flops, bytes_accessed=16 * mats * rows * dim, transcendentals=0),
        compiler_params=pltpu.CompilerParams(
            collective_id=0, has_side_effects=True, vmem_limit_bytes=58 * 1024 * 1024
        ),
    )


def make_finish(n_zero, mats, rows, dim):
    hid = rows * n_zero

    def kernel(table, nm, update, nm_out, up_out, own_out, nm_in, nm_wide, up, own, sems):
        me = lax.axis_index("zero")
        rows_mine = update.at[:, pl.ds(pl.multiple_of(me * rows, 16), rows), :]
        nm_load = pltpu.make_async_copy(nm, nm_in, sems.at[0])
        nm_load.start()
        up_load = pltpu.make_async_copy(rows_mine, up, sems.at[1])
        up_load.start()
        count = jnp.int32(0)
        for j in range(mats):
            owned = table[j] == me
            count = count + owned.astype(jnp.int32)

            @pl.when(owned)
            def _():
                pltpu.make_async_copy(update.at[j], own, sems.at[2]).start()

        nm_load.wait()
        nm_store = []
        for j in range(mats):
            nm_wide[j] = nm_in[j].astype(jnp.float32)
            nm_store.append(pltpu.make_async_copy(nm_wide.at[j], nm_out.at[j], sems.at[5 + j]))
            nm_store[j].start()
        up_load.wait()
        up_store = pltpu.make_async_copy(up, up_out, sems.at[3])
        up_store.start()

        @pl.when(count == 0)
        def _():
            own[...] = jnp.zeros(own.shape, own.dtype)

        @pl.when(count > 0)
        def _():
            pltpu.make_async_copy(update.at[0], own, sems.at[2]).wait()

        own_store = pltpu.make_async_copy(own, own_out.at[0], sems.at[4])
        own_store.start()
        up_store.wait()
        own_store.wait()
        for j in range(mats):
            nm_store[j].wait()

    return pl.pallas_call(
        kernel,
        out_shape=(
            jax.ShapeDtypeStruct((mats, rows, dim), jnp.float32),
            jax.ShapeDtypeStruct((mats, rows, dim), jnp.bfloat16),
            jax.ShapeDtypeStruct((1, hid, dim), jnp.bfloat16),
        ),
        in_specs=[
            pl.BlockSpec(memory_space=pltpu.SMEM),
            pl.BlockSpec(memory_space=pl.ANY),
            pl.BlockSpec(memory_space=pl.ANY),
        ],
        out_specs=(pl.BlockSpec(memory_space=pl.ANY),) * 3,
        scratch_shapes=[
            pltpu.VMEM((mats, rows, dim), jnp.bfloat16),
            pltpu.VMEM((mats, rows, dim), jnp.float32),
            pltpu.VMEM((mats, rows, dim), jnp.bfloat16),
            pltpu.VMEM((hid, dim), jnp.bfloat16),
            pltpu.SemaphoreType.DMA((5 + mats,)),
        ],
        cost_estimate=pl.CostEstimate(flops=0, bytes_accessed=16 * mats * rows * dim, transcendentals=0),
        compiler_params=pltpu.CompilerParams(vmem_limit_bytes=58 * 1024 * 1024),
    )


def solution(mesh):
    n_dp, n_zero = mesh.shape["dp"], mesh.shape["zero"]

    def kernel_step(grad_parts, momentum, owner_table):
        _, mats, rows, dim = grad_parts.shape
        nm, update = make_kernel(n_dp, n_zero, mats, rows, dim)(grad_parts, momentum)
        return make_finish(n_zero, mats, rows, dim)(owner_table, nm, update)

    def on_device(grad_parts, momentum, owner_table):
        _, mats, rows, dim = grad_parts.shape
        fits = (
            mats == 3
            and n_zero == 4
            and n_dp % 2 == 0
            and n_dp >= 4
            and dim % (LANES * n_dp) == 0
            and dim % 256 == 0
            and rows % 16 == 0
        )
        body = kernel_step if fits else general_step
        return body(grad_parts, momentum, owner_table)

    placed = (P("dp", None, "zero", None), P(None, "zero", None), P())
    return jax.shard_map(
        on_device,
        mesh=mesh,
        in_specs=placed,
        out_specs=(P(None, "zero", None), P(None, "zero", None), P("zero", None, None)),
        check_vma=False,
    )
```

```python
import math

import jax
import jax.numpy as jnp
from jax import lax
from jax.experimental import pallas as pl
from jax.experimental.pallas import tpu as pltpu
from jax.sharding import PartitionSpec as P

ITERS = 2
COEF_A = 3.4445
COEF_B = -4.775
COEF_C = 2.0315
MOMENTUM_DECAY = 0.95
NORM_EPSILON = 1e-07
MESH = pl.DeviceIdType.MESH
LANES = 128


def orthogonalize(matrix):
    current = matrix
    iterate = matrix.astype(jnp.float32)
    for step in range(ITERS):
        gram_matrix = jnp.dot(current, current.T, preferred_element_type=jnp.float32).astype(
            jnp.bfloat16
        )
        squared = jnp.dot(gram_matrix, gram_matrix, preferred_element_type=jnp.float32)
        poly_term = (COEF_B * gram_matrix.astype(jnp.float32) + COEF_C * squared).astype(
            jnp.bfloat16
        )
        iterate = COEF_A * current.astype(jnp.float32) + jnp.dot(
            poly_term, current, preferred_element_type=jnp.float32
        )
        if step + 1 < ITERS:
            current = iterate.astype(jnp.bfloat16)
    return (0.2 * math.sqrt(matrix.shape[1]) * iterate).astype(jnp.bfloat16)


def general_step(grad_parts, momentum, owner_table):
    my_index = lax.axis_index("zero")
    local_part = grad_parts[0].astype(jnp.float32)
    summed = lax.psum(local_part, "dp")
    new_momentum = MOMENTUM_DECAY * momentum + summed
    partial_value = jnp.sum(new_momentum * new_momentum, axis=(1, 2))
    squares = lax.psum(partial_value, "zero")
    inverse = 1.0 / (jnp.sqrt(squares) + NORM_EPSILON)
    start_rows = (new_momentum * inverse[:, None, None]).astype(jnp.bfloat16)
    mine_mask = (owner_table == my_index).astype(jnp.bfloat16)
    gathered = lax.all_gather(start_rows, "zero", axis=1, tiled=True)
    full_matrix = jnp.einsum(
        "j,jrd->rd", mine_mask, gathered, preferred_element_type=jnp.float32
    ).astype(jnp.bfloat16)
    result = orthogonalize(full_matrix)
    contrib = mine_mask.astype(jnp.float32)[:, None, None] * result.astype(jnp.float32)[None]
    update_rows = lax.psum_scatter(
        contrib.astype(jnp.bfloat16), "zero", scatter_dimension=1, tiled=True
    )
    return (new_momentum, update_rows, result[None])


def column_tiles(width, step=256):
    return [(at, min(step, width - at)) for at in range(0, width, step)]


def make_kernel(n_dp, n_zero, mats, rows, dim):
    hid = rows * n_zero
    half = hid // 2
    gram_tiles = len(column_tiles(hid))
    wide = 512 if dim % 512 == 0 else 256
    n_line = n_dp // 2
    width = dim // n_dp
    out_scale = 0.2 * math.sqrt(dim)

    def kernel(
        grad, momentum, nm_out, up_out,
        grads, stage, pairs_in, pairs, x, full, later, gram, parts, mom, poly, scale,
        ra_s, ra_r, rs_s, rs_r, s1_s, s1_r, s2_s, s2_r, s3_s, s3_r, s4_s, s4_r, gx_s, gx_r, xx_s, xx_r, local,
    ):
        d = lax.axis_index("dp")
        o = lax.axis_index("zero")
        zi, xi, yi, ci = d // 2, d % 2, o // 2, o % 2
        x_peer = zi * 2 + 1 - xi
        y_peer = (1 - yi) * 2 + ci
        c_peer = yi * 2 + 1 - ci

        def row(s):
            return pl.ds(pl.multiple_of(s * rows, 16), rows)

        def col(k):
            return pl.ds(pl.multiple_of(k * width, LANES), width)

        def chunk(j, s, k):
            return x.at[j, k, row(s), :]

        def line(r):
            return (zi + n_line - r) % n_line

        def remote(src, dst, send, recv, to):
            return pltpu.make_async_remote_copy(
                src_ref=src, dst_ref=dst, send_sem=send, recv_sem=recv,
                device_id=to, device_id_type=MESH,
            )

        def ra(j, r):
            k = ((zi + r) % n_line) * 2 + 1 - xi
            return remote(stage.at[j, k], pairs_in.at[j, r], ra_s.at[j, r], ra_r.at[j, r], (x_peer, o))

        def rb(j, r):
            to = (((zi + r) % n_line) * 2 + xi, o)
            return remote(pairs.at[j, r - 1], parts.at[j, r - 1], rs_s.at[j, r], rs_r.at[j, r], to)

        def s1(j, r):
            c = chunk(j, o, d)
            return remote(c, c, s1_s.at[j, r], s1_r.at[j, r], (((zi + r) % n_line) * 2 + xi, o))

        def s1_in(j, r):
            c = chunk(j, o, line(r) * 2 + xi)
            return remote(c, c, s1_s.at[j, r], s1_r.at[j, r], (((zi + r) % n_line) * 2 + xi, o))

        def s2(j, r):
            c = chunk(j, o, line(r) * 2 + xi)
            return remote(c, c, s2_s.at[j, r], s2_r.at[j, r], (x_peer, o))

        def s2_in(j, r):
            c = chunk(j, o, line(r) * 2 + 1 - xi)
            return remote(c, c, s2_s.at[j, r], s2_r.at[j, r], (x_peer, o))

        def s3(j, r, h, s=None):
            k = line(r) * 2 + (xi if h == 0 else 1 - xi)
            c = chunk(j, o if s is None else s, k)
            return remote(c, c, s3_s.at[j, r, h], s3_r.at[j, r, h], (d, y_peer))

        def s3_in(j, r, h):
            return s3(j, r, h, y_peer)

        def s4(j, h, s=None):
            if s is None:
                s = o if h == 0 else y_peer
            c = x.at[j, :, row(s), :]
            return remote(c, c, s4_s.at[j, h], s4_r.at[j, h], (d, c_peer))

        def s4_in(j, h):
            return s4(j, h, c_peer if h == 0 else (1 - yi) * 2 + 1 - ci)

        def load_grad(j):
            return pltpu.make_async_copy(grad.at[0, j], grads.at[j], local.at[j])

        def own_momentum():
            return pltpu.make_async_copy(momentum.at[:, :, col(d)], mom, local.at[mats])

        def nm_copy(j):
            return pltpu.make_async_copy(full.at[j, row(o), :], nm_out.at[j], local.at[mats + 1 + j])

        def up_copy(j):
            return pltpu.make_async_copy(later.at[ITERS - 1, j], up_out.at[j], local.at[2 * mats + 1 + j])

        peers = [(((zi + r) % n_line) * 2 + xi, o) for r in range(1, n_line)]
        peers += [(x_peer, o), (d, y_peer), (d, c_peer)]
        barrier = pltpu.get_barrier_semaphore()
        for j in range(mats):
            load_grad(j).start()
        own_momentum().start()
        for to in peers:
            pl.semaphore_signal(barrier, inc=1, device_id=to, device_id_type=MESH)

        def put_together(j):
            load_grad(j).wait()
            for k in range(n_dp):
                stage[j, k] = grads[j, :, k * width : (k + 1) * width]

        def send_parts(j):
            for r in [*range(1, n_line), 0]:
                ra(j, r).start()

        def pair(j, r):
            k = ((zi + r) % n_line) * 2 + xi
            return stage[j, k].astype(jnp.float32) + pairs_in[j, r].astype(jnp.float32)

        def phase_p(j):
            for r in range(1, n_line):
                ra(j, r).wait_recv()
                pairs[j, r - 1] = pair(j, r).astype(jnp.bfloat16)
                rb(j, r).start()

        def phase_a(j):
            if j == 0:
                own_momentum().wait()
            ra(j, 0).wait_recv()
            for r in range(1, n_line):
                rb(j, r).wait_recv()
            total = pair(j, 0)
            for r in range(n_line - 1):
                total = total + parts[j, r].astype(jnp.float32)
            x[j, d, row(o), :] = (MOMENTUM_DECAY * mom[j] + total).astype(jnp.bfloat16)
            s3(j, 0, 0).start()
            s2(j, 0).start()
            for r in range(1, n_line):
                s1(j, r).start()

        def phase_b(j):
            for r in range(1, n_line):
                s1_in(j, r).wait_recv()
                s2(j, r).start()
                s3(j, r, 0).start()

        def phase_c(j):
            for r in range(n_line):
                s2_in(j, r).wait_recv()
                s3(j, r, 1).start()
            s4(j, 0).start()

        def phase_d(j):
            for r in range(n_line):
                for h in range(2):
                    s3_in(j, r, h).wait_recv()
            s4(j, 1).start()

        def phase_e(j):
            for h in range(2):
                s4_in(j, h).wait_recv()

        def half_rows(c):
            return pl.ds(pl.multiple_of(c * half, 16), half)

        def gx(j, it, n, c=None):
            at, size = column_tiles(hid)[n]
            g = gram.at[j, it, half_rows(ci if c is None else c), at : at + size]
            return remote(g, g, gx_s.at[j, it, n], gx_r.at[j, it, n], (d, c_peer))

        def xx(j, it, n, c=None):
            cols = slice(n * wide, (n + 1) * wide)
            v = later.at[it, j, half_rows(ci if c is None else c), cols]
            return remote(v, v, xx_s.at[j, it, n], xx_r.at[j, it, n], (d, c_peer))

        def gx_wait(j, it):
            for n in range(gram_tiles):
                gx(j, it, n, 1 - ci).wait_recv()

        def xx_wait(j, it):
            for n in range(dim // wide):
                xx(j, it, n, 1 - ci).wait_recv()

        mine = half_rows(ci)

        def source(j, it):
            return full.at[j] if it == 0 else later.at[it - 1, j]

        def gram_op(j, it):
            src = source(j, it)
            if it == 0:
                acc = jnp.zeros((1, width), jnp.float32)
                for k in range(n_dp):
                    v = x[j, k]
                    full[j, :, k * width : (k + 1) * width] = v
                    w = v.astype(jnp.float32)
                    acc = acc + jnp.sum(w * w, axis=0, keepdims=True)
                nm_copy(j).start()
                total = jnp.sum(acc, axis=1, keepdims=True)
                scale[j] = jnp.broadcast_to(1.0 / (jnp.sqrt(total) + NORM_EPSILON), scale.shape[1:])
            else:
                xx_wait(j, it - 1)
            g = lax.dot_general(
                src[mine, :], src[...], (((1,), (1,)), ((), ())),
                preferred_element_type=jnp.float32,
            )
            if it == 0:
                s = scale[j, 0:1, 0:1]
                g = g * s * s
            gram[j, it, mine, :] = g.astype(jnp.bfloat16)
            for n in range(gram_tiles):
                gx(j, it, n).start()

        def apply_op(j, it):
            src = source(j, it)
            gx_wait(j, it)
            q = jnp.dot(gram[j, it, mine, :], gram[j, it], preferred_element_type=jnp.float32)
            own = gram[j, it, mine, :].astype(jnp.float32)
            poly[...] = (COEF_B * own + COEF_C * q).astype(jnp.bfloat16)
            for n in range(dim // wide):
                cols = slice(n * wide, (n + 1) * wide)
                y = COEF_A * src[mine, cols].astype(jnp.float32) + jnp.dot(
                    poly[...], src[:, cols], preferred_element_type=jnp.float32
                )
                if it == 0:
                    y = y * scale[j, 0:1, 0:1]
                if it == ITERS - 1:
                    y = y * out_scale
                later[it, j, mine, cols] = y.astype(jnp.bfloat16)
                xx(j, it, n).start()

        def finish(j):
            xx_wait(j, ITERS - 1)
            up_copy(j).start()

        put_together(0)
        pl.semaphore_wait(barrier, len(peers))
        for j in range(mats):
            if j > 0:
                put_together(j)
            send_parts(j)
        phase_p(0)
        phase_p(1)
        phase_a(0)
        phase_p(2)
        phase_a(1)
        phase_b(0)
        phase_c(0)
        phase_a(2)
        phase_b(1)
        phase_d(0)
        phase_c(1)
        phase_b(2)
        phase_e(0)
        gram_op(0, 0)
        phase_c(2)
        phase_d(1)
        apply_op(0, 0)
        phase_e(1)
        gram_op(1, 0)
        phase_d(2)
        gram_op(0, 1)
        apply_op(1, 0)
        phase_e(2)
        gram_op(2, 0)
        apply_op(0, 1)
        gram_op(1, 1)
        apply_op(2, 0)
        finish(0)
        apply_op(1, 1)
        gram_op(2, 1)
        finish(1)
        apply_op(2, 1)
        finish(2)

        for j in range(mats):
            for r in range(n_line):
                ra(j, r).wait_send()
            for r in range(1, n_line):
                rb(j, r).wait_send()
                s1(j, r).wait_send()
            for r in range(n_line):
                s2(j, r).wait_send()
                for h in range(2):
                    s3(j, r, h).wait_send()
            for h in range(2):
                s4(j, h).wait_send()
            for it in range(ITERS):
                for n in range(gram_tiles):
                    gx(j, it, n).wait_send()
                for n in range(dim // wide):
                    xx(j, it, n).wait_send()
            nm_copy(j).wait()
            up_copy(j).wait()

    dma = pltpu.SemaphoreType.DMA
    flops = mats * ITERS * hid * hid * (2 * dim + hid)
    return pl.pallas_call(
        kernel,
        out_shape=(
            jax.ShapeDtypeStruct((mats, rows, dim), jnp.bfloat16),
            jax.ShapeDtypeStruct((mats, hid, dim), jnp.bfloat16),
        ),
        in_specs=[pl.BlockSpec(memory_space=pl.ANY)] * 2,
        out_specs=(pl.BlockSpec(memory_space=pl.ANY),) * 2,
        scratch_shapes=[
            pltpu.VMEM((mats, rows, dim), jnp.bfloat16),
            pltpu.VMEM((mats, n_dp, rows, width), jnp.bfloat16),
            pltpu.VMEM((mats, n_line, rows, width), jnp.bfloat16),
            pltpu.VMEM((mats, n_line - 1, rows, width), jnp.bfloat16),
            pltpu.VMEM((mats, n_dp, hid, width), jnp.bfloat16),
            pltpu.VMEM((mats, hid, dim), jnp.bfloat16),
            pltpu.VMEM((ITERS, mats, hid, dim), jnp.bfloat16),
            pltpu.VMEM((mats, ITERS, hid, hid), jnp.bfloat16),
            pltpu.VMEM((mats, n_line - 1, rows, width), jnp.bfloat16),
            pltpu.VMEM((mats, rows, width), jnp.float32),
            pltpu.VMEM((half, hid), jnp.bfloat16),
            pltpu.VMEM((mats, 8, LANES), jnp.float32),
            dma((mats, n_line)), dma((mats, n_line)),
            dma((mats, n_line)), dma((mats, n_line)),
            dma((mats, n_line)), dma((mats, n_line)),
            dma((mats, n_line)), dma((mats, n_line)),
            dma((mats, n_line, 2)), dma((mats, n_line, 2)),
            dma((mats, 2)), dma((mats, 2)),
            dma((mats, ITERS, gram_tiles)), dma((mats, ITERS, gram_tiles)),
            dma((mats, ITERS, dim // wide)), dma((mats, ITERS, dim // wide)),
            dma((3 * mats + 1,)),
        ],
        cost_estimate=pl.CostEstimate(flops=flops, bytes_accessed=16 * mats * rows * dim, transcendentals=0),
        compiler_params=pltpu.CompilerParams(
            collective_id=0, has_side_effects=True, vmem_limit_bytes=58 * 1024 * 1024
        ),
    )


def make_finish(n_zero, mats, rows, dim):
    hid = rows * n_zero

    def kernel(table, nm, update, nm_out, up_out, own_out, nm_in, nm_wide, up, own, sems):
        me = lax.axis_index("zero")
        rows_mine = pl.ds(pl.multiple_of(me * rows, 16), rows)
        copy = pltpu.make_async_copy

        def part(q):
            return pl.ds(q * rows, rows)

        def own_load(j, q):
            return copy(update.at[j, part(q), :], own.at[part(q), :], sems.at[2, q])

        nm_load = [copy(nm.at[j], nm_in.at[j], sems.at[0, j]) for j in range(mats)]
        up_load = [copy(update.at[j, rows_mine, :], up.at[j], sems.at[1, j]) for j in range(mats)]
        nm_store = [copy(nm_wide.at[j], nm_out.at[j], sems.at[3, j]) for j in range(mats)]
        up_store = [copy(up.at[j], up_out.at[j], sems.at[4, j]) for j in range(mats)]
        own_store = [copy(own.at[part(q), :], own_out.at[0, part(q), :], sems.at[5, q]) for q in range(n_zero)]
        for load in nm_load + up_load:
            load.start()
        count = jnp.int32(0)
        for j in range(mats):
            owned = table[j] == me
            count = count + owned.astype(jnp.int32)

            @pl.when(owned)
            def _():
                for q in range(n_zero):
                    own_load(j, q).start()

        for j in range(mats):
            nm_load[j].wait()
            nm_wide[j] = nm_in[j].astype(jnp.float32)
            nm_store[j].start()
        for j in range(mats):
            up_load[j].wait()
            up_store[j].start()

        @pl.when(count == 0)
        def _():
            own[...] = jnp.zeros(own.shape, own.dtype)

        for q in range(n_zero):

            @pl.when(count > 0)
            def _():
                own_load(0, q).wait()

            own_store[q].start()
        for store in nm_store + up_store + own_store:
            store.wait()

    return pl.pallas_call(
        kernel,
        out_shape=(
            jax.ShapeDtypeStruct((mats, rows, dim), jnp.float32),
            jax.ShapeDtypeStruct((mats, rows, dim), jnp.bfloat16),
            jax.ShapeDtypeStruct((1, hid, dim), jnp.bfloat16),
        ),
        in_specs=[
            pl.BlockSpec(memory_space=pltpu.SMEM),
            pl.BlockSpec(memory_space=pl.ANY),
            pl.BlockSpec(memory_space=pl.ANY),
        ],
        out_specs=(pl.BlockSpec(memory_space=pl.ANY),) * 3,
        scratch_shapes=[
            pltpu.VMEM((mats, rows, dim), jnp.bfloat16),
            pltpu.VMEM((mats, rows, dim), jnp.float32),
            pltpu.VMEM((mats, rows, dim), jnp.bfloat16),
            pltpu.VMEM((hid, dim), jnp.bfloat16),
            pltpu.SemaphoreType.DMA((6, max(mats, n_zero))),
        ],
        cost_estimate=pl.CostEstimate(flops=0, bytes_accessed=16 * mats * rows * dim, transcendentals=0),
        compiler_params=pltpu.CompilerParams(vmem_limit_bytes=58 * 1024 * 1024),
    )


def solution(mesh):
    n_dp, n_zero = mesh.shape["dp"], mesh.shape["zero"]

    def kernel_step(grad_parts, momentum, owner_table):
        _, mats, rows, dim = grad_parts.shape
        nm, update = make_kernel(n_dp, n_zero, mats, rows, dim)(grad_parts, momentum)
        return make_finish(n_zero, mats, rows, dim)(owner_table, nm, update)

    def on_device(grad_parts, momentum, owner_table):
        _, mats, rows, dim = grad_parts.shape
        fits = (
            mats == 3
            and n_zero == 4
            and n_dp % 2 == 0
            and n_dp >= 4
            and dim % (LANES * n_dp) == 0
            and dim % 256 == 0
            and rows % 16 == 0
        )
        body = kernel_step if fits else general_step
        return body(grad_parts, momentum, owner_table)

    placed = (P("dp", None, "zero", None), P(None, "zero", None), P())
    return jax.shard_map(
        on_device,
        mesh=mesh,
        in_specs=placed,
        out_specs=(P(None, "zero", None), P(None, "zero", None), P("zero", None, None)),
        check_vma=False,
    )
```

```python
import math

import jax
import jax.numpy as jnp
from jax import lax
from jax.experimental import pallas as pl
from jax.experimental.pallas import tpu as pltpu
from jax.sharding import PartitionSpec as P

ITERS = 2
COEF_A = 3.4445
COEF_B = -4.775
COEF_C = 2.0315
MOMENTUM_DECAY = 0.95
NORM_EPSILON = 1e-07
MESH = pl.DeviceIdType.MESH
LANES = 128


def orthogonalize(matrix):
    current = matrix
    iterate = matrix.astype(jnp.float32)
    for step in range(ITERS):
        gram_matrix = jnp.dot(current, current.T, preferred_element_type=jnp.float32).astype(
            jnp.bfloat16
        )
        squared = jnp.dot(gram_matrix, gram_matrix, preferred_element_type=jnp.float32)
        poly_term = (COEF_B * gram_matrix.astype(jnp.float32) + COEF_C * squared).astype(
            jnp.bfloat16
        )
        iterate = COEF_A * current.astype(jnp.float32) + jnp.dot(
            poly_term, current, preferred_element_type=jnp.float32
        )
        if step + 1 < ITERS:
            current = iterate.astype(jnp.bfloat16)
    return (0.2 * math.sqrt(matrix.shape[1]) * iterate).astype(jnp.bfloat16)


def general_step(grad_parts, momentum, owner_table):
    my_index = lax.axis_index("zero")
    local_part = grad_parts[0].astype(jnp.float32)
    summed = lax.psum(local_part, "dp")
    new_momentum = MOMENTUM_DECAY * momentum + summed
    partial_value = jnp.sum(new_momentum * new_momentum, axis=(1, 2))
    squares = lax.psum(partial_value, "zero")
    inverse = 1.0 / (jnp.sqrt(squares) + NORM_EPSILON)
    start_rows = (new_momentum * inverse[:, None, None]).astype(jnp.bfloat16)
    mine_mask = (owner_table == my_index).astype(jnp.bfloat16)
    gathered = lax.all_gather(start_rows, "zero", axis=1, tiled=True)
    full_matrix = jnp.einsum(
        "j,jrd->rd", mine_mask, gathered, preferred_element_type=jnp.float32
    ).astype(jnp.bfloat16)
    result = orthogonalize(full_matrix)
    contrib = mine_mask.astype(jnp.float32)[:, None, None] * result.astype(jnp.float32)[None]
    update_rows = lax.psum_scatter(
        contrib.astype(jnp.bfloat16), "zero", scatter_dimension=1, tiled=True
    )
    return (new_momentum, update_rows, result[None])


def column_tiles(width, step=256):
    return [(at, min(step, width - at)) for at in range(0, width, step)]


def make_kernel(n_dp, n_zero, mats, rows, dim):
    hid = rows * n_zero
    half = hid // 2
    gram_tiles = len(column_tiles(hid))
    wide = 512 if dim % 512 == 0 else 256
    n_line = n_dp // 2
    width = dim // n_dp
    out_scale = 0.2 * math.sqrt(dim)

    def kernel(
        grad, momentum, nm_out, up_out,
        grads, stage, pairs_in, pairs, x, full, later, gram, parts, mom, poly, scale,
        ra_s, ra_r, rs_s, rs_r, s1_s, s1_r, s2_s, s2_r, s3_s, s3_r, s4_s, s4_r, gx_s, gx_r, xx_s, xx_r, local,
    ):
        d = lax.axis_index("dp")
        o = lax.axis_index("zero")
        zi, xi, yi, ci = d // 2, d % 2, o // 2, o % 2
        x_peer = zi * 2 + 1 - xi
        y_peer = (1 - yi) * 2 + ci
        c_peer = yi * 2 + 1 - ci

        def row(s):
            return pl.ds(pl.multiple_of(s * rows, 16), rows)

        def col(k):
            return pl.ds(pl.multiple_of(k * width, LANES), width)

        def chunk(j, s, k):
            return x.at[j, k, row(s), :]

        def line(r):
            return (zi + n_line - r) % n_line

        def remote(src, dst, send, recv, to):
            return pltpu.make_async_remote_copy(
                src_ref=src, dst_ref=dst, send_sem=send, recv_sem=recv,
                device_id=to, device_id_type=MESH,
            )

        def ra(j, r):
            k = ((zi + r) % n_line) * 2 + 1 - xi
            return remote(stage.at[j, k], pairs_in.at[j, r], ra_s.at[j, r], ra_r.at[j, r], (x_peer, o))

        def rb(j, r):
            to = (((zi + r) % n_line) * 2 + xi, o)
            return remote(pairs.at[j, r - 1], parts.at[j, r - 1], rs_s.at[j, r], rs_r.at[j, r], to)

        def s1(j, r):
            c = chunk(j, o, d)
            return remote(c, c, s1_s.at[j, r], s1_r.at[j, r], (((zi + r) % n_line) * 2 + xi, o))

        def s1_in(j, r):
            c = chunk(j, o, line(r) * 2 + xi)
            return remote(c, c, s1_s.at[j, r], s1_r.at[j, r], (((zi + r) % n_line) * 2 + xi, o))

        def s2(j, r):
            c = chunk(j, o, line(r) * 2 + xi)
            return remote(c, c, s2_s.at[j, r], s2_r.at[j, r], (x_peer, o))

        def s2_in(j, r):
            c = chunk(j, o, line(r) * 2 + 1 - xi)
            return remote(c, c, s2_s.at[j, r], s2_r.at[j, r], (x_peer, o))

        def s3(j, r, h, s=None):
            k = line(r) * 2 + (xi if h == 0 else 1 - xi)
            c = chunk(j, o if s is None else s, k)
            return remote(c, c, s3_s.at[j, r, h], s3_r.at[j, r, h], (d, y_peer))

        def s3_in(j, r, h):
            return s3(j, r, h, y_peer)

        def s4(j, h, s=None):
            if s is None:
                s = o if h == 0 else y_peer
            c = x.at[j, :, row(s), :]
            return remote(c, c, s4_s.at[j, h], s4_r.at[j, h], (d, c_peer))

        def s4_in(j, h):
            return s4(j, h, c_peer if h == 0 else (1 - yi) * 2 + 1 - ci)

        def load_grad(j):
            return pltpu.make_async_copy(grad.at[0, j], grads.at[j], local.at[j])

        def own_momentum():
            return pltpu.make_async_copy(momentum.at[:, :, col(d)], mom, local.at[mats])

        def nm_copy(j):
            return pltpu.make_async_copy(full.at[j, row(o), :], nm_out.at[j], local.at[mats + 1 + j])

        def up_copy(j, c):
            part = pl.ds(pl.multiple_of(c * half, 16), half)
            sem = local.at[2 * mats + 1 + j] if c is ci else local.at[3 * mats + 1 + j]
            return pltpu.make_async_copy(later.at[ITERS - 1, j, part, :], up_out.at[j, part, :], sem)

        peers = [(((zi + r) % n_line) * 2 + xi, o) for r in range(1, n_line)]
        peers += [(x_peer, o), (d, y_peer), (d, c_peer)]
        barrier = pltpu.get_barrier_semaphore()
        for j in range(mats):
            load_grad(j).start()
        own_momentum().start()
        for to in peers:
            pl.semaphore_signal(barrier, inc=1, device_id=to, device_id_type=MESH)

        def put_together(j):
            load_grad(j).wait()
            for k in range(n_dp):
                stage[j, k] = grads[j, :, k * width : (k + 1) * width]

        def send_parts(j):
            for r in [*range(1, n_line), 0]:
                ra(j, r).start()

        def pair(j, r):
            k = ((zi + r) % n_line) * 2 + xi
            return stage[j, k].astype(jnp.float32) + pairs_in[j, r].astype(jnp.float32)

        def phase_p(j):
            for r in range(1, n_line):
                ra(j, r).wait_recv()
                pairs[j, r - 1] = pair(j, r).astype(jnp.bfloat16)
                rb(j, r).start()

        def phase_a(j):
            if j == 0:
                own_momentum().wait()
            ra(j, 0).wait_recv()
            for r in range(1, n_line):
                rb(j, r).wait_recv()
            total = pair(j, 0)
            for r in range(n_line - 1):
                total = total + parts[j, r].astype(jnp.float32)
            x[j, d, row(o), :] = (MOMENTUM_DECAY * mom[j] + total).astype(jnp.bfloat16)
            s3(j, 0, 0).start()
            s2(j, 0).start()
            for r in range(1, n_line):
                s1(j, r).start()

        def phase_b(j):
            for r in range(1, n_line):
                s1_in(j, r).wait_recv()
                s2(j, r).start()
                s3(j, r, 0).start()

        def phase_c(j):
            for r in range(n_line):
                s2_in(j, r).wait_recv()
                s3(j, r, 1).start()
            s4(j, 0).start()

        def phase_d(j):
            for r in range(n_line):
                for h in range(2):
                    s3_in(j, r, h).wait_recv()
            s4(j, 1).start()

        def phase_e(j):
            for h in range(2):
                s4_in(j, h).wait_recv()

        def half_rows(c):
            return pl.ds(pl.multiple_of(c * half, 16), half)

        def gx(j, it, n, c=None):
            at, size = column_tiles(hid)[n]
            g = gram.at[j, it, half_rows(ci if c is None else c), at : at + size]
            return remote(g, g, gx_s.at[j, it, n], gx_r.at[j, it, n], (d, c_peer))

        def xx(j, it, n, c=None):
            cols = slice(n * wide, (n + 1) * wide)
            v = later.at[it, j, half_rows(ci if c is None else c), cols]
            return remote(v, v, xx_s.at[j, it, n], xx_r.at[j, it, n], (d, c_peer))

        def gx_wait(j, it):
            for n in range(gram_tiles):
                gx(j, it, n, 1 - ci).wait_recv()

        def xx_wait(j, it):
            for n in range(dim // wide):
                xx(j, it, n, 1 - ci).wait_recv()

        mine = half_rows(ci)

        def source(j, it):
            return full.at[j] if it == 0 else later.at[it - 1, j]

        def gram_op(j, it):
            src = source(j, it)
            if it == 0:
                acc = jnp.zeros((1, width), jnp.float32)
                for k in range(n_dp):
                    v = x[j, k]
                    full[j, :, k * width : (k + 1) * width] = v
                    w = v.astype(jnp.float32)
                    acc = acc + jnp.sum(w * w, axis=0, keepdims=True)
                nm_copy(j).start()
                total = jnp.sum(acc, axis=1, keepdims=True)
                scale[j] = jnp.broadcast_to(1.0 / (jnp.sqrt(total) + NORM_EPSILON), scale.shape[1:])
            else:
                xx_wait(j, it - 1)
            g = lax.dot_general(
                src[mine, :], src[...], (((1,), (1,)), ((), ())),
                preferred_element_type=jnp.float32,
            )
            if it == 0:
                s = scale[j, 0:1, 0:1]
                g = g * s * s
            gram[j, it, mine, :] = g.astype(jnp.bfloat16)
            for n in range(gram_tiles):
                gx(j, it, n).start()

        def apply_op(j, it):
            src = source(j, it)
            gx_wait(j, it)
            q = jnp.dot(gram[j, it, mine, :], gram[j, it], preferred_element_type=jnp.float32)
            own = gram[j, it, mine, :].astype(jnp.float32)
            poly[...] = (COEF_B * own + COEF_C * q).astype(jnp.bfloat16)
            for n in range(dim // wide):
                cols = slice(n * wide, (n + 1) * wide)
                y = COEF_A * src[mine, cols].astype(jnp.float32) + jnp.dot(
                    poly[...], src[:, cols], preferred_element_type=jnp.float32
                )
                if it == 0:
                    y = y * scale[j, 0:1, 0:1]
                if it == ITERS - 1:
                    y = y * out_scale
                later[it, j, mine, cols] = y.astype(jnp.bfloat16)
                xx(j, it, n).start()
            if it == ITERS - 1:
                up_copy(j, ci).start()

        def finish(j):
            xx_wait(j, ITERS - 1)
            up_copy(j, 1 - ci).start()

        put_together(0)
        pl.semaphore_wait(barrier, len(peers))
        for j in range(mats):
            if j > 0:
                put_together(j)
            send_parts(j)
        phase_p(0)
        phase_p(1)
        phase_a(0)
        phase_p(2)
        phase_a(1)
        phase_b(0)
        phase_c(0)
        phase_a(2)
        phase_b(1)
        phase_d(0)
        phase_e(0)
        gram_op(0, 0)
        phase_c(1)
        phase_b(2)
        apply_op(0, 0)
        phase_c(2)
        phase_d(1)
        phase_e(1)
        gram_op(1, 0)
        gram_op(0, 1)
        phase_d(2)
        apply_op(1, 0)
        apply_op(0, 1)
        phase_e(2)
        gram_op(2, 0)
        gram_op(1, 1)
        finish(0)
        apply_op(2, 0)
        apply_op(1, 1)
        gram_op(2, 1)
        finish(1)
        apply_op(2, 1)
        finish(2)

        for j in range(mats):
            for r in range(n_line):
                ra(j, r).wait_send()
            for r in range(1, n_line):
                rb(j, r).wait_send()
                s1(j, r).wait_send()
            for r in range(n_line):
                s2(j, r).wait_send()
                for h in range(2):
                    s3(j, r, h).wait_send()
            for h in range(2):
                s4(j, h).wait_send()
            for it in range(ITERS):
                for n in range(gram_tiles):
                    gx(j, it, n).wait_send()
                for n in range(dim // wide):
                    xx(j, it, n).wait_send()
            nm_copy(j).wait()
            up_copy(j, ci).wait()
            up_copy(j, 1 - ci).wait()

    dma = pltpu.SemaphoreType.DMA
    flops = mats * ITERS * hid * hid * (2 * dim + hid)
    return pl.pallas_call(
        kernel,
        out_shape=(
            jax.ShapeDtypeStruct((mats, rows, dim), jnp.bfloat16),
            jax.ShapeDtypeStruct((mats, hid, dim), jnp.bfloat16),
        ),
        in_specs=[pl.BlockSpec(memory_space=pl.ANY)] * 2,
        out_specs=(pl.BlockSpec(memory_space=pl.ANY),) * 2,
        scratch_shapes=[
            pltpu.VMEM((mats, rows, dim), jnp.bfloat16),
            pltpu.VMEM((mats, n_dp, rows, width), jnp.bfloat16),
            pltpu.VMEM((mats, n_line, rows, width), jnp.bfloat16),
            pltpu.VMEM((mats, n_line - 1, rows, width), jnp.bfloat16),
            pltpu.VMEM((mats, n_dp, hid, width), jnp.bfloat16),
            pltpu.VMEM((mats, hid, dim), jnp.bfloat16),
            pltpu.VMEM((ITERS, mats, hid, dim), jnp.bfloat16),
            pltpu.VMEM((mats, ITERS, hid, hid), jnp.bfloat16),
            pltpu.VMEM((mats, n_line - 1, rows, width), jnp.bfloat16),
            pltpu.VMEM((mats, rows, width), jnp.float32),
            pltpu.VMEM((half, hid), jnp.bfloat16),
            pltpu.VMEM((mats, 8, LANES), jnp.float32),
            dma((mats, n_line)), dma((mats, n_line)),
            dma((mats, n_line)), dma((mats, n_line)),
            dma((mats, n_line)), dma((mats, n_line)),
            dma((mats, n_line)), dma((mats, n_line)),
            dma((mats, n_line, 2)), dma((mats, n_line, 2)),
            dma((mats, 2)), dma((mats, 2)),
            dma((mats, ITERS, gram_tiles)), dma((mats, ITERS, gram_tiles)),
            dma((mats, ITERS, dim // wide)), dma((mats, ITERS, dim // wide)),
            dma((4 * mats + 1,)),
        ],
        cost_estimate=pl.CostEstimate(flops=flops, bytes_accessed=16 * mats * rows * dim, transcendentals=0),
        compiler_params=pltpu.CompilerParams(
            collective_id=0, has_side_effects=True, vmem_limit_bytes=58 * 1024 * 1024
        ),
    )


def make_finish(n_zero, mats, rows, dim):
    hid = rows * n_zero

    def kernel(table, nm, update, nm_out, up_out, own_out, nm_in, nm_wide, up, own, sems):
        me = lax.axis_index("zero")
        rows_mine = pl.ds(pl.multiple_of(me * rows, 16), rows)
        copy = pltpu.make_async_copy

        def part(q):
            return pl.ds(q * rows, rows)

        def own_load(j, q):
            return copy(update.at[j, part(q), :], own.at[part(q), :], sems.at[2, q])

        nm_load = [copy(nm.at[j], nm_in.at[j], sems.at[0, j]) for j in range(mats)]
        up_load = [copy(update.at[j, rows_mine, :], up.at[j], sems.at[1, j]) for j in range(mats)]
        nm_store = [copy(nm_wide.at[j], nm_out.at[j], sems.at[3, j]) for j in range(mats)]
        up_store = [copy(up.at[j], up_out.at[j], sems.at[4, j]) for j in range(mats)]
        own_store = [copy(own.at[part(q), :], own_out.at[0, part(q), :], sems.at[5, q]) for q in range(n_zero)]
        for load in nm_load + up_load:
            load.start()
        count = jnp.int32(0)
        for j in range(mats):
            owned = table[j] == me
            count = count + owned.astype(jnp.int32)

            @pl.when(owned)
            def _():
                for q in range(n_zero):
                    own_load(j, q).start()

        for j in range(mats):
            nm_load[j].wait()
            nm_wide[j] = nm_in[j].astype(jnp.float32)
            nm_store[j].start()
        for j in range(mats):
            up_load[j].wait()
            up_store[j].start()

        @pl.when(count == 0)
        def _():
            own[...] = jnp.zeros(own.shape, own.dtype)

        for q in range(n_zero):

            @pl.when(count > 0)
            def _():
                own_load(0, q).wait()

            own_store[q].start()
        for store in nm_store + up_store + own_store:
            store.wait()

    return pl.pallas_call(
        kernel,
        out_shape=(
            jax.ShapeDtypeStruct((mats, rows, dim), jnp.float32),
            jax.ShapeDtypeStruct((mats, rows, dim), jnp.bfloat16),
            jax.ShapeDtypeStruct((1, hid, dim), jnp.bfloat16),
        ),
        in_specs=[
            pl.BlockSpec(memory_space=pltpu.SMEM),
            pl.BlockSpec(memory_space=pl.ANY),
            pl.BlockSpec(memory_space=pl.ANY),
        ],
        out_specs=(pl.BlockSpec(memory_space=pl.ANY),) * 3,
        scratch_shapes=[
            pltpu.VMEM((mats, rows, dim), jnp.bfloat16),
            pltpu.VMEM((mats, rows, dim), jnp.float32),
            pltpu.VMEM((mats, rows, dim), jnp.bfloat16),
            pltpu.VMEM((hid, dim), jnp.bfloat16),
            pltpu.SemaphoreType.DMA((6, max(mats, n_zero))),
        ],
        cost_estimate=pl.CostEstimate(flops=0, bytes_accessed=16 * mats * rows * dim, transcendentals=0),
        compiler_params=pltpu.CompilerParams(vmem_limit_bytes=58 * 1024 * 1024),
    )


def solution(mesh):
    n_dp, n_zero = mesh.shape["dp"], mesh.shape["zero"]

    def kernel_step(grad_parts, momentum, owner_table):
        _, mats, rows, dim = grad_parts.shape
        nm, update = make_kernel(n_dp, n_zero, mats, rows, dim)(grad_parts, momentum)
        return make_finish(n_zero, mats, rows, dim)(owner_table, nm, update)

    def on_device(grad_parts, momentum, owner_table):
        _, mats, rows, dim = grad_parts.shape
        fits = (
            mats == 3
            and n_zero == 4
            and n_dp % 2 == 0
            and n_dp >= 4
            and dim % (LANES * n_dp) == 0
            and dim % 256 == 0
            and rows % 16 == 0
        )
        body = kernel_step if fits else general_step
        return body(grad_parts, momentum, owner_table)

    placed = (P("dp", None, "zero", None), P(None, "zero", None), P())
    return jax.shard_map(
        on_device,
        mesh=mesh,
        in_specs=placed,
        out_specs=(P(None, "zero", None), P(None, "zero", None), P("zero", None, None)),
        check_vma=False,
    )
```

```python
import math

import jax
import jax.numpy as jnp
from jax import lax
from jax.experimental import pallas as pl
from jax.experimental.pallas import tpu as pltpu
from jax.sharding import PartitionSpec as P

ITERS = 2
COEF_A = 3.4445
COEF_B = -4.775
COEF_C = 2.0315
MOMENTUM_DECAY = 0.95
NORM_EPSILON = 1e-07
MESH = pl.DeviceIdType.MESH
LANES = 128


def orthogonalize(matrix):
    current = matrix
    iterate = matrix.astype(jnp.float32)
    for step in range(ITERS):
        gram_matrix = jnp.dot(current, current.T, preferred_element_type=jnp.float32).astype(
            jnp.bfloat16
        )
        squared = jnp.dot(gram_matrix, gram_matrix, preferred_element_type=jnp.float32)
        poly_term = (COEF_B * gram_matrix.astype(jnp.float32) + COEF_C * squared).astype(
            jnp.bfloat16
        )
        iterate = COEF_A * current.astype(jnp.float32) + jnp.dot(
            poly_term, current, preferred_element_type=jnp.float32
        )
        if step + 1 < ITERS:
            current = iterate.astype(jnp.bfloat16)
    return (0.2 * math.sqrt(matrix.shape[1]) * iterate).astype(jnp.bfloat16)


def general_step(grad_parts, momentum, owner_table):
    my_index = lax.axis_index("zero")
    local_part = grad_parts[0].astype(jnp.float32)
    summed = lax.psum(local_part, "dp")
    new_momentum = MOMENTUM_DECAY * momentum + summed
    partial_value = jnp.sum(new_momentum * new_momentum, axis=(1, 2))
    squares = lax.psum(partial_value, "zero")
    inverse = 1.0 / (jnp.sqrt(squares) + NORM_EPSILON)
    start_rows = (new_momentum * inverse[:, None, None]).astype(jnp.bfloat16)
    mine_mask = (owner_table == my_index).astype(jnp.bfloat16)
    gathered = lax.all_gather(start_rows, "zero", axis=1, tiled=True)
    full_matrix = jnp.einsum(
        "j,jrd->rd", mine_mask, gathered, preferred_element_type=jnp.float32
    ).astype(jnp.bfloat16)
    result = orthogonalize(full_matrix)
    contrib = mine_mask.astype(jnp.float32)[:, None, None] * result.astype(jnp.float32)[None]
    update_rows = lax.psum_scatter(
        contrib.astype(jnp.bfloat16), "zero", scatter_dimension=1, tiled=True
    )
    return (new_momentum, update_rows, result[None])


def column_tiles(width, step=256):
    return [(at, min(step, width - at)) for at in range(0, width, step)]


def make_kernel(n_dp, n_zero, mats, rows, dim):
    hid = rows * n_zero
    half = hid // 2
    gram_tiles = len(column_tiles(hid))
    wide = 512 if dim % 512 == 0 else 256
    n_line = n_dp // 2
    width = dim // n_dp
    out_scale = 0.2 * math.sqrt(dim)

    def kernel(
        grad, momentum, nm_out, up_out,
        grads, stage, pairs_in, pairs, x, full, later, gram, parts, mom, poly, scale,
        ra_s, ra_r, rs_s, rs_r, s1_s, s1_r, s2_s, s2_r, s3_s, s3_r, s4_s, s4_r, gx_s, gx_r, xx_s, xx_r, local,
    ):
        d = lax.axis_index("dp")
        o = lax.axis_index("zero")
        zi, xi, yi, ci = d // 2, d % 2, o // 2, o % 2
        x_peer = zi * 2 + 1 - xi
        y_peer = (1 - yi) * 2 + ci
        c_peer = yi * 2 + 1 - ci

        def row(s):
            return pl.ds(pl.multiple_of(s * rows, 16), rows)

        def col(k):
            return pl.ds(pl.multiple_of(k * width, LANES), width)

        def chunk(j, s, k):
            return x.at[j, k, row(s), :]

        def line(r):
            return (zi + n_line - r) % n_line

        def remote(src, dst, send, recv, to):
            return pltpu.make_async_remote_copy(
                src_ref=src, dst_ref=dst, send_sem=send, recv_sem=recv,
                device_id=to, device_id_type=MESH,
            )

        def ra(j, r):
            k = ((zi + r) % n_line) * 2 + 1 - xi
            return remote(stage.at[j, k], pairs_in.at[j, r], ra_s.at[j, r], ra_r.at[j, r], (x_peer, o))

        def rb(j, r):
            to = (((zi + r) % n_line) * 2 + xi, o)
            return remote(pairs.at[j, r - 1], parts.at[j, r - 1], rs_s.at[j, r], rs_r.at[j, r], to)

        def s1(j, r):
            c = chunk(j, o, d)
            return remote(c, c, s1_s.at[j, r], s1_r.at[j, r], (((zi + r) % n_line) * 2 + xi, o))

        def s1_in(j, r):
            c = chunk(j, o, line(r) * 2 + xi)
            return remote(c, c, s1_s.at[j, r], s1_r.at[j, r], (((zi + r) % n_line) * 2 + xi, o))

        def s2(j, r):
            c = chunk(j, o, line(r) * 2 + xi)
            return remote(c, c, s2_s.at[j, r], s2_r.at[j, r], (x_peer, o))

        def s2_in(j, r):
            c = chunk(j, o, line(r) * 2 + 1 - xi)
            return remote(c, c, s2_s.at[j, r], s2_r.at[j, r], (x_peer, o))

        def s3(j, r, h, s=None):
            k = line(r) * 2 + (xi if h == 0 else 1 - xi)
            c = chunk(j, o if s is None else s, k)
            return remote(c, c, s3_s.at[j, r, h], s3_r.at[j, r, h], (d, y_peer))

        def s3_in(j, r, h):
            return s3(j, r, h, y_peer)

        def s4(j, h, s=None):
            if s is None:
                s = o if h == 0 else y_peer
            c = x.at[j, :, row(s), :]
            return remote(c, c, s4_s.at[j, h], s4_r.at[j, h], (d, c_peer))

        def s4_in(j, h):
            return s4(j, h, c_peer if h == 0 else (1 - yi) * 2 + 1 - ci)

        def load_grad(j):
            return pltpu.make_async_copy(grad.at[0, j], grads.at[j], local.at[j])

        def own_momentum():
            return pltpu.make_async_copy(momentum.at[:, :, col(d)], mom, local.at[mats])

        def nm_copy(j):
            return pltpu.make_async_copy(full.at[j, row(o), :], nm_out.at[j], local.at[mats + 1 + j])

        def up_copy(j, c):
            part = pl.ds(pl.multiple_of(c * half, 16), half)
            sem = local.at[2 * mats + 1 + j] if c is ci else local.at[3 * mats + 1 + j]
            return pltpu.make_async_copy(later.at[ITERS - 1, j, part, :], up_out.at[j, part, :], sem)

        peers = [(((zi + r) % n_line) * 2 + xi, o) for r in range(1, n_line)]
        peers += [(x_peer, o), (d, y_peer), (d, c_peer)]
        barrier = pltpu.get_barrier_semaphore()
        for j in range(mats):
            load_grad(j).start()
        own_momentum().start()
        for to in peers:
            pl.semaphore_signal(barrier, inc=1, device_id=to, device_id_type=MESH)

        def put_together(j):
            load_grad(j).wait()
            for k in range(n_dp):
                stage[j, k] = grads[j, :, k * width : (k + 1) * width]

        def send_parts(j):
            for r in [*range(1, n_line), 0]:
                ra(j, r).start()

        def pair(j, r):
            k = ((zi + r) % n_line) * 2 + xi
            return stage[j, k].astype(jnp.float32) + pairs_in[j, r].astype(jnp.float32)

        def phase_p(j):
            for r in range(1, n_line):
                ra(j, r).wait_recv()
                pairs[j, r - 1] = pair(j, r).astype(jnp.bfloat16)
                rb(j, r).start()

        def phase_a(j):
            if j == 0:
                own_momentum().wait()
            ra(j, 0).wait_recv()
            for r in range(1, n_line):
                rb(j, r).wait_recv()
            total = pair(j, 0)
            for r in range(n_line - 1):
                total = total + parts[j, r].astype(jnp.float32)
            x[j, d, row(o), :] = (MOMENTUM_DECAY * mom[j] + total).astype(jnp.bfloat16)
            for r in range(1, n_line):
                s1(j, r).start()
            s3(j, 0, 0).start()
            s2(j, 0).start()

        def phase_b(j):
            for r in range(1, n_line):
                s1_in(j, r).wait_recv()
                s2(j, r).start()
                s3(j, r, 0).start()

        def phase_c(j):
            for r in range(n_line):
                s2_in(j, r).wait_recv()
                s3(j, r, 1).start()
            s4(j, 0).start()

        def phase_d(j):
            for r in range(n_line):
                for h in range(2):
                    s3_in(j, r, h).wait_recv()
            s4(j, 1).start()

        def phase_e(j):
            for h in range(2):
                s4_in(j, h).wait_recv()

        def half_rows(c):
            return pl.ds(pl.multiple_of(c * half, 16), half)

        def gx(j, it, n, c=None):
            at, size = column_tiles(hid)[n]
            g = gram.at[j, it, half_rows(ci if c is None else c), at : at + size]
            return remote(g, g, gx_s.at[j, it, n], gx_r.at[j, it, n], (d, c_peer))

        def xx(j, it, n, c=None):
            cols = slice(n * wide, (n + 1) * wide)
            v = later.at[it, j, half_rows(ci if c is None else c), cols]
            return remote(v, v, xx_s.at[j, it, n], xx_r.at[j, it, n], (d, c_peer))

        def gx_wait(j, it):
            for n in range(gram_tiles):
                gx(j, it, n, 1 - ci).wait_recv()

        def xx_wait(j, it):
            for n in range(dim // wide):
                xx(j, it, n, 1 - ci).wait_recv()

        mine = half_rows(ci)

        def source(j, it):
            return full.at[j] if it == 0 else later.at[it - 1, j]

        def gram_op(j, it):
            src = source(j, it)
            if it == 0:
                acc = jnp.zeros((1, width), jnp.float32)
                for k in range(n_dp):
                    v = x[j, k]
                    full[j, :, k * width : (k + 1) * width] = v
                    w = v.astype(jnp.float32)
                    acc = acc + jnp.sum(w * w, axis=0, keepdims=True)
                nm_copy(j).start()
                total = jnp.sum(acc, axis=1, keepdims=True)
                scale[j] = jnp.broadcast_to(1.0 / (jnp.sqrt(total) + NORM_EPSILON), scale.shape[1:])
            else:
                xx_wait(j, it - 1)
            g = lax.dot_general(
                src[mine, :], src[...], (((1,), (1,)), ((), ())),
                preferred_element_type=jnp.float32,
            )
            if it == 0:
                s = scale[j, 0:1, 0:1]
                g = g * s * s
            gram[j, it, mine, :] = g.astype(jnp.bfloat16)
            for n in range(gram_tiles):
                gx(j, it, n).start()

        def apply_op(j, it):
            src = source(j, it)
            gx_wait(j, it)
            q = jnp.dot(gram[j, it, mine, :], gram[j, it], preferred_element_type=jnp.float32)
            own = gram[j, it, mine, :].astype(jnp.float32)
            poly[...] = (COEF_B * own + COEF_C * q).astype(jnp.bfloat16)
            for n in range(dim // wide):
                cols = slice(n * wide, (n + 1) * wide)
                y = COEF_A * src[mine, cols].astype(jnp.float32) + jnp.dot(
                    poly[...], src[:, cols], preferred_element_type=jnp.float32
                )
                if it == 0:
                    y = y * scale[j, 0:1, 0:1]
                if it == ITERS - 1:
                    y = y * out_scale
                later[it, j, mine, cols] = y.astype(jnp.bfloat16)
                xx(j, it, n).start()
            if it == ITERS - 1:
                up_copy(j, ci).start()

        def finish(j):
            xx_wait(j, ITERS - 1)
            up_copy(j, 1 - ci).start()

        put_together(0)
        pl.semaphore_wait(barrier, len(peers))
        for j in range(mats):
            if j > 0:
                put_together(j)
            send_parts(j)
        phase_p(0)
        phase_p(1)
        phase_a(0)
        phase_p(2)
        phase_a(1)
        phase_b(0)
        phase_c(0)
        phase_a(2)
        phase_b(1)
        phase_d(0)
        phase_c(1)
        phase_b(2)
        phase_e(0)
        gram_op(0, 0)
        phase_c(2)
        phase_d(1)
        apply_op(0, 0)
        phase_e(1)
        gram_op(1, 0)
        phase_d(2)
        gram_op(0, 1)
        apply_op(1, 0)
        phase_e(2)
        gram_op(2, 0)
        apply_op(0, 1)
        gram_op(1, 1)
        apply_op(2, 0)
        finish(0)
        apply_op(1, 1)
        gram_op(2, 1)
        finish(1)
        apply_op(2, 1)
        finish(2)

        for j in range(mats):
            for r in range(n_line):
                ra(j, r).wait_send()
            for r in range(1, n_line):
                rb(j, r).wait_send()
                s1(j, r).wait_send()
            for r in range(n_line):
                s2(j, r).wait_send()
                for h in range(2):
                    s3(j, r, h).wait_send()
            for h in range(2):
                s4(j, h).wait_send()
            for it in range(ITERS):
                for n in range(gram_tiles):
                    gx(j, it, n).wait_send()
                for n in range(dim // wide):
                    xx(j, it, n).wait_send()
            nm_copy(j).wait()
            up_copy(j, ci).wait()
            up_copy(j, 1 - ci).wait()

    dma = pltpu.SemaphoreType.DMA
    flops = mats * ITERS * hid * hid * (2 * dim + hid)
    return pl.pallas_call(
        kernel,
        out_shape=(
            jax.ShapeDtypeStruct((mats, rows, dim), jnp.bfloat16),
            jax.ShapeDtypeStruct((mats, hid, dim), jnp.bfloat16),
        ),
        in_specs=[pl.BlockSpec(memory_space=pl.ANY)] * 2,
        out_specs=(pl.BlockSpec(memory_space=pl.ANY),) * 2,
        scratch_shapes=[
            pltpu.VMEM((mats, rows, dim), jnp.bfloat16),
            pltpu.VMEM((mats, n_dp, rows, width), jnp.bfloat16),
            pltpu.VMEM((mats, n_line, rows, width), jnp.bfloat16),
            pltpu.VMEM((mats, n_line - 1, rows, width), jnp.bfloat16),
            pltpu.VMEM((mats, n_dp, hid, width), jnp.bfloat16),
            pltpu.VMEM((mats, hid, dim), jnp.bfloat16),
            pltpu.VMEM((ITERS, mats, hid, dim), jnp.bfloat16),
            pltpu.VMEM((mats, ITERS, hid, hid), jnp.bfloat16),
            pltpu.VMEM((mats, n_line - 1, rows, width), jnp.bfloat16),
            pltpu.VMEM((mats, rows, width), jnp.float32),
            pltpu.VMEM((half, hid), jnp.bfloat16),
            pltpu.VMEM((mats, 8, LANES), jnp.float32),
            dma((mats, n_line)), dma((mats, n_line)),
            dma((mats, n_line)), dma((mats, n_line)),
            dma((mats, n_line)), dma((mats, n_line)),
            dma((mats, n_line)), dma((mats, n_line)),
            dma((mats, n_line, 2)), dma((mats, n_line, 2)),
            dma((mats, 2)), dma((mats, 2)),
            dma((mats, ITERS, gram_tiles)), dma((mats, ITERS, gram_tiles)),
            dma((mats, ITERS, dim // wide)), dma((mats, ITERS, dim // wide)),
            dma((4 * mats + 1,)),
        ],
        cost_estimate=pl.CostEstimate(flops=flops, bytes_accessed=16 * mats * rows * dim, transcendentals=0),
        compiler_params=pltpu.CompilerParams(
            collective_id=0, has_side_effects=True, vmem_limit_bytes=58 * 1024 * 1024
        ),
    )


def make_finish(n_zero, mats, rows, dim):
    hid = rows * n_zero

    def kernel(table, nm, update, nm_out, up_out, own_out, nm_in, nm_wide, up, own, sems):
        me = lax.axis_index("zero")
        rows_mine = pl.ds(pl.multiple_of(me * rows, 16), rows)
        copy = pltpu.make_async_copy

        def part(q):
            return pl.ds(q * rows, rows)

        def own_load(j, q):
            return copy(update.at[j, part(q), :], own.at[part(q), :], sems.at[2, q])

        nm_load = [copy(nm.at[j], nm_in.at[j], sems.at[0, j]) for j in range(mats)]
        up_load = [copy(update.at[j, rows_mine, :], up.at[j], sems.at[1, j]) for j in range(mats)]
        nm_store = [copy(nm_wide.at[j], nm_out.at[j], sems.at[3, j]) for j in range(mats)]
        up_store = [copy(up.at[j], up_out.at[j], sems.at[4, j]) for j in range(mats)]
        own_store = [copy(own.at[part(q), :], own_out.at[0, part(q), :], sems.at[5, q]) for q in range(n_zero)]
        for load in nm_load + up_load:
            load.start()
        count = jnp.int32(0)
        for j in range(mats):
            owned = table[j] == me
            count = count + owned.astype(jnp.int32)

            @pl.when(owned)
            def _():
                for q in range(n_zero):
                    own_load(j, q).start()

        for j in range(mats):
            nm_load[j].wait()
            nm_wide[j] = nm_in[j].astype(jnp.float32)
            nm_store[j].start()
        for j in range(mats):
            up_load[j].wait()
            up_store[j].start()

        @pl.when(count == 0)
        def _():
            own[...] = jnp.zeros(own.shape, own.dtype)

        for q in range(n_zero):

            @pl.when(count > 0)
            def _():
                own_load(0, q).wait()

            own_store[q].start()
        for store in nm_store + up_store + own_store:
            store.wait()

    return pl.pallas_call(
        kernel,
        out_shape=(
            jax.ShapeDtypeStruct((mats, rows, dim), jnp.float32),
            jax.ShapeDtypeStruct((mats, rows, dim), jnp.bfloat16),
            jax.ShapeDtypeStruct((1, hid, dim), jnp.bfloat16),
        ),
        in_specs=[
            pl.BlockSpec(memory_space=pltpu.SMEM),
            pl.BlockSpec(memory_space=pl.ANY),
            pl.BlockSpec(memory_space=pl.ANY),
        ],
        out_specs=(pl.BlockSpec(memory_space=pl.ANY),) * 3,
        scratch_shapes=[
            pltpu.VMEM((mats, rows, dim), jnp.bfloat16),
            pltpu.VMEM((mats, rows, dim), jnp.float32),
            pltpu.VMEM((mats, rows, dim), jnp.bfloat16),
            pltpu.VMEM((hid, dim), jnp.bfloat16),
            pltpu.SemaphoreType.DMA((6, max(mats, n_zero))),
        ],
        cost_estimate=pl.CostEstimate(flops=0, bytes_accessed=16 * mats * rows * dim, transcendentals=0),
        compiler_params=pltpu.CompilerParams(vmem_limit_bytes=58 * 1024 * 1024),
    )


def solution(mesh):
    n_dp, n_zero = mesh.shape["dp"], mesh.shape["zero"]

    def kernel_step(grad_parts, momentum, owner_table):
        _, mats, rows, dim = grad_parts.shape
        nm, update = make_kernel(n_dp, n_zero, mats, rows, dim)(grad_parts, momentum)
        return make_finish(n_zero, mats, rows, dim)(owner_table, nm, update)

    def on_device(grad_parts, momentum, owner_table):
        _, mats, rows, dim = grad_parts.shape
        fits = (
            mats == 3
            and n_zero == 4
            and n_dp % 2 == 0
            and n_dp >= 4
            and dim % (LANES * n_dp) == 0
            and dim % 256 == 0
            and rows % 16 == 0
        )
        body = kernel_step if fits else general_step
        return body(grad_parts, momentum, owner_table)

    placed = (P("dp", None, "zero", None), P(None, "zero", None), P())
    return jax.shard_map(
        on_device,
        mesh=mesh,
        in_specs=placed,
        out_specs=(P(None, "zero", None), P(None, "zero", None), P("zero", None, None)),
        check_vma=False,
    )
```
